512 devices in a mesh: ctx: 256 (over y_lo, x, z, core), head: 2 (over y_hi).
Axes of the slice: x: 4, y: 4 (y_hi: 2, y_lo: 2; y = y_hi * 2 + y_lo), z: 16, core: 2. Of those that a mesh axis runs over, the one named last changes fastest.
Arguments:
- queries: bfloat16 [32768, 1536], P('ctx', 'head'), may hold values from -8 to 8
- key_states: bfloat16 [32768, 1536], P('ctx', 'head'), may hold values from -8 to 8
- value_states: bfloat16 [32768, 1536], P('ctx', 'head'), may hold values from -6 to 6
- out_grad: bfloat16 [32768, 1536], P('ctx', 'head'), may hold values from -24 to 24
- rel_table: bfloat16 [256, 128], replicated, may hold values from -3 to 3
- block_mask: int32 [256, 3], P('ctx'), may hold values 0 or 1
- distance_shift: int32 [256, 3], P('ctx'), may hold values from 0 to 127
Outputs:
- query_grad: bfloat16 [32768, 1536], P('ctx', 'head')
- key_grad: bfloat16 [32768, 1536], P('ctx', 'head')
- value_grad: bfloat16 [32768, 1536], P('ctx', 'head')
- table_grad: float32 [256, 128], replicated
The draws below stay inside these ranges and needn't reach their ends.
All inputs are finite; a program needn't handle non-finite values. No bound on the sum of `block_mask` on one device may be relied on, other than what follows from the above.
Results may differ from the reference program's by a relative error of at most 0.033.
Values may be sent and summed in bfloat16 or wider, within the bound.
No kernel may reach another device: no remote copies, remote signals or barrier semaphores. Data moves between devices by JAX's collectives and lax.ppermute only.
A program may use at most 64 MiB of HBM per device.

```python
from functools import reduce
import jax
import jax.numpy as jnp
from jax import lax

HEADS = 12
HEAD_DIM = 128
TOK_DEV = 128
NSTEP = 3
BLOCKS = 256
TOKENS = 32768
NREL = 256


def draw_queries(key, part):
    key = jax.random.fold_in(key, 1)
    shape = (TOKENS, HEADS * HEAD_DIM)
    values = jnp.clip(jax.random.normal(key, shape, jnp.float32), -8.0, 8.0)
    return values.astype(jnp.bfloat16)


def draw_key_states(key, part):
    key = jax.random.fold_in(key, 2)
    shape = (TOKENS, HEADS * HEAD_DIM)
    values = jnp.clip(jax.random.normal(key, shape, jnp.float32), -8.0, 8.0)
    return values.astype(jnp.bfloat16)


def with_ends(result, rng, smallest, top_value):
    dims = result.shape
    index_at = [jax.random.randint(jax.random.fold_in(rng, axis), (), 0, dims[axis]) for axis in range(len(dims))]
    result = result.at[tuple(index_at)].set(smallest)
    longest = dims.index(max(dims))
    index_at[longest] = (index_at[longest] + 1) % dims[longest]
    return result.at[tuple(index_at)].set(top_value)


def levels(stream_key, dims, split, low, top_value):
    level = 1.0
    for axis_at, parts in split:
        steps = jax.random.uniform(jax.random.fold_in(jax.random.fold_in(stream_key, 6), axis_at), (parts,), jnp.float32, low / len(split), top_value / len(split))
        level = level * jnp.repeat(jnp.exp(steps), dims[axis_at] // parts).reshape((-1,) + (1,) * (len(dims) - 1 - axis_at))
    return level


def centred(own_key, dims, scale, reach, pieces=(), kind=jnp.bfloat16):
    loudness = levels(own_key, dims, pieces, -0.22, 0.18) if pieces else 1.0
    array = jax.random.normal(own_key, dims, jnp.float32) * scale * loudness
    return jnp.minimum(jnp.maximum(array, -reach), reach).astype(kind)


def setup_inputs(seed: int = 0) -> dict:
    streams_of = jax.random.split(jax.random.key(seed), 8)
    queries = draw_queries(jax.random.fold_in(streams_of[7], 71), 0)
    key_states = draw_key_states(jax.random.fold_in(streams_of[7], 71), 0)
    value_states = centred(streams_of[2], (TOKENS, HEADS * HEAD_DIM), 1.0, 6.0, ((0, 256), (1, 2)))
    out_grad = centred(streams_of[3], (TOKENS, HEADS * HEAD_DIM), 4.0, 24.0, ((0, 256), (1, 2)))
    rel_table = centred(streams_of[4], (NREL, HEAD_DIM), 0.5, 3.0)
    block_mask = with_ends((jax.random.randint(streams_of[5], (BLOCKS, NSTEP), 0, 4) < 3).astype(jnp.int32), jax.random.fold_in(streams_of[5], 1), 0, 1)
    distance_shift = with_ends(jax.random.randint(streams_of[6], (BLOCKS, NSTEP), 0, TOK_DEV), jax.random.fold_in(streams_of[6], 1), 0, TOK_DEV - 1).astype(jnp.int32)
    return {"queries": queries, "key_states": key_states, "value_states": value_states, "out_grad": out_grad, "rel_table": rel_table, "block_mask": block_mask, "distance_shift": distance_shift}


def skewed(block):
    width = block.shape[-2]
    lead = block.shape[:-2]
    flipped = jnp.flip(block[..., :2 * width - 1], axis=-1)
    padded = jnp.concatenate([flipped, jnp.zeros(lead + (width, 1), block.dtype)], axis=-1)
    flat = padded.reshape(lead + (2 * width * width,))[..., :width * (2 * width - 1)]
    return flat.reshape(lead + (width, 2 * width - 1))[..., width - 1:2 * width - 1]

def unskewed(grad_block):
    width = grad_block.shape[-1]
    shape = grad_block.shape[:-1] + (2 * width,)
    _, pullback = jax.vjp(skewed, jnp.zeros(shape, grad_block.dtype))
    return pullback(grad_block)[0]

def padded_table(rel_table, width):
    first = jnp.broadcast_to(rel_table[:1], (2 * width, rel_table.shape[1]))
    last = jnp.broadcast_to(rel_table[-1:], (2 * width, rel_table.shape[1]))
    return jnp.concatenate([first, rel_table, last], axis=0)

def window_rows(table, offset, step, width):
    start = (step * width + width + 1 - offset).astype(jnp.int32)
    return (lax.dynamic_slice_in_dim(table, start, 2 * width, 0), start)

def folded_table(padded_grad, width, rows):
    middle = padded_grad[2 * width:2 * width + rows]
    low = lax.optimization_barrier(jnp.sum(padded_grad[:2 * width], axis=0))
    high = lax.optimization_barrier(jnp.sum(padded_grad[2 * width + rows:], axis=0))
    middle = middle.at[0].add(low)
    return middle.at[rows - 1].add(high)

def block_terms(query, grads_out, key_list, value_list, table, mask_row, shift_row, block_id):
    width = query.shape[0]
    scale = query.shape[2] ** (-0.5)
    steps = len(key_list)
    lower = jnp.arange(width)[None, :] <= jnp.arange(width)[:, None]
    query_f = query.astype(jnp.float32)
    grads_f = grads_out.astype(jnp.float32)
    scores, seen_list, windows, starts = ([], [], [], [])
    for step in range(steps):
        rows_w, start = window_rows(table, shift_row[step], step, width)
        if step == 0:
            seen = lower
        else:
            seen = jnp.broadcast_to((mask_row[step] == 1) & (block_id >= step), (width, width))
        content = jnp.einsum('ihd,jhd->hij', query_f, key_list[step].astype(jnp.float32))
        relative = jnp.einsum('ihd,ud->hiu', query_f, rows_w.astype(jnp.float32))
        scores.append(scale * (content + skewed(relative)))
        seen_list.append(seen)
        windows.append(rows_w)
        starts.append(start)
    top = reduce(jnp.maximum, [lax.optimization_barrier(jnp.max(jnp.where(s[None], x, -jnp.inf), axis=-1)) for x, s in zip(scores, seen_list)])
    total = sum([lax.optimization_barrier(jnp.sum(jnp.where(s[None], jnp.exp(x - top[..., None]), 0.0), axis=-1)) for x, s in zip(scores, seen_list)])
    lse = top + jnp.log(total)
    probs = [jnp.where(s[None], jnp.exp(x - lse[..., None]), 0.0) for x, s in zip(scores, seen_list)]
    weights = [p.astype(jnp.bfloat16) for p in probs]
    output = sum([jnp.einsum('hij,jhd->ihd', w.astype(jnp.float32), v.astype(jnp.float32)) for w, v in zip(weights, value_list)])
    output = output.astype(jnp.bfloat16)
    delta = jnp.einsum('ihd,ihd->hi', grads_f, output.astype(jnp.float32))
    query_acc = jnp.zeros(query.shape, jnp.float32)
    table_acc = jnp.zeros(table.shape, jnp.float32)
    key_parts, value_parts = ([], [])
    for step in range(steps):
        dprob = jnp.einsum('ihd,jhd->hij', grads_f, value_list[step].astype(jnp.float32))
        dscore = (scale * probs[step] * (dprob - delta[..., None])).astype(jnp.bfloat16)
        dscore_f = dscore.astype(jnp.float32)
        rel_grad = unskewed(dscore).astype(jnp.float32)
        query_acc = query_acc + jnp.einsum('hij,jhd->ihd', dscore_f, key_list[step].astype(jnp.float32))
        query_acc = query_acc + jnp.einsum('hiu,ud->ihd', rel_grad, windows[step].astype(jnp.float32))
        rows_grad = jnp.einsum('hiu,ihd->ud', rel_grad, query_f)
        current = lax.dynamic_slice_in_dim(table_acc, starts[step], 2 * width, 0)
        table_acc = lax.dynamic_update_slice_in_dim(table_acc, current + rows_grad, starts[step], 0)
        key_parts.append(jnp.einsum('hij,ihd->jhd', dscore_f, query_f))
        value_parts.append(jnp.einsum('hij,ihd->jhd', weights[step].astype(jnp.float32), grads_f))
    return (query_acc, table_acc, key_parts, value_parts)

def reference(queries, key_states, value_states, out_grad, rel_table, block_mask, distance_shift):
    width = TOK_DEV
    steps = NSTEP
    blocks = BLOCKS
    shape_b = (blocks, width, HEADS, HEAD_DIM)
    table = padded_table(rel_table, width)
    query_all = queries.reshape(shape_b)
    grads_all = out_grad.reshape(shape_b)
    lead = jnp.zeros((steps - 1, width, HEADS, HEAD_DIM), key_states.dtype)
    key_pad = jnp.concatenate([lead, key_states.reshape(shape_b)], axis=0)
    value_pad = jnp.concatenate([lead, value_states.reshape(shape_b)], axis=0)

    def visit(carry, block_id):
        key_acc, value_acc, table_sum = carry
        query = lax.dynamic_index_in_dim(query_all, block_id, 0, keepdims=False)
        grads_out = lax.dynamic_index_in_dim(grads_all, block_id, 0, keepdims=False)
        key_win = lax.dynamic_slice_in_dim(key_pad, block_id, steps, 0)
        value_win = lax.dynamic_slice_in_dim(value_pad, block_id, steps, 0)
        key_list = [key_win[steps - 1 - step] for step in range(steps)]
        value_list = [value_win[steps - 1 - step] for step in range(steps)]
        mask_row = lax.dynamic_index_in_dim(block_mask, block_id, 0, keepdims=False)
        shift_row = lax.dynamic_index_in_dim(distance_shift, block_id, 0, keepdims=False)
        query_acc, table_acc, key_parts, value_parts = block_terms(query, grads_out, key_list, value_list, table, mask_row, shift_row, block_id)
        key_stack = jnp.stack(key_parts[::-1])
        value_stack = jnp.stack(value_parts[::-1])
        key_acc = lax.dynamic_update_slice_in_dim(key_acc, lax.dynamic_slice_in_dim(key_acc, block_id, steps, 0) + key_stack, block_id, 0)
        value_acc = lax.dynamic_update_slice_in_dim(value_acc, lax.dynamic_slice_in_dim(value_acc, block_id, steps, 0) + value_stack, block_id, 0)
        return ((key_acc, value_acc, table_sum + table_acc), query_acc.astype(jnp.bfloat16))
    acc_shape = (blocks + steps - 1, width, HEADS, HEAD_DIM)
    init = (jnp.zeros(acc_shape, jnp.float32), jnp.zeros(acc_shape, jnp.float32), jnp.zeros(table.shape, jnp.float32))
    carry, query_blocks = lax.scan(visit, init, jnp.arange(blocks, dtype=jnp.int32))
    key_acc, value_acc, table_sum = carry
    full = (blocks * width, HEADS * HEAD_DIM)
    query_grad = query_blocks.reshape(full)
    key_grad = key_acc[steps - 1:].reshape(full).astype(jnp.bfloat16)
    value_grad = value_acc[steps - 1:].reshape(full).astype(jnp.bfloat16)
    table_grad = folded_table(table_sum, width, NREL)
    return (query_grad, key_grad, value_grad, table_grad)
```

```python
import jax
import jax.numpy as jnp
from jax import lax
from jax.experimental import pallas as pl
from jax.experimental.pallas import tpu as pltpu
from jax.sharding import PartitionSpec as P

HEAD_DIM = 128
AXES = ("ctx", "head")
NT = (((1,), (1,)), ((), ()))
TN = (((0,), (0,)), ((), ()))


def dot(a, b, dims=(((1,), (0,)), ((), ()))):
    return lax.dot_general(a, b, dims, preferred_element_type=jnp.float32)


def lanes(values, index):
    return jnp.take_along_axis(values, index, axis=1, mode="promise_in_bounds")


def block_kernel(
    block_ref, mask_ref, shift_ref, query_ref, grad_ref, key_ref, value_ref, far_ref, pair_ref,
    cross_ref, table_ref, query_out, own_out, near_out, far_out, table_out, near_kv
):
    width = query_ref.shape[0]
    heads = query_ref.shape[1] // HEAD_DIM
    rows = table_ref.shape[0]
    scale = HEAD_DIM ** (-0.5)
    block = block_ref[0]
    odd = lax.rem(block, 2) == 1

    @pl.when(odd)
    def _():
        near_kv[...] = pair_ref[0]

    @pl.when(jnp.logical_not(odd))
    def _():
        near_kv[...] = cross_ref[1]

    row = lax.broadcasted_iota(jnp.int32, (width, width), 0)
    col = lax.broadcasted_iota(jnp.int32, (width, width), 1)
    bases = [step * width - shift_ref[0, step] for step in range(3)]
    seen = col <= row
    biases = [
        jnp.where((mask_ref[0, step] == 1) & (block >= step), 0.0, -jnp.inf) for step in (1, 2)
    ]
    place = [col - row + (rows - 1) - base for base in bases]
    high = [place[0] > rows - 1, place[1] > rows - 1]
    low = place[2] < 0
    place = [jnp.clip(item, 0, rows - 1) for item in place]
    upper = [item >= width for item in place]
    place = [item & (width - 1) for item in place]
    source = [col + row - (rows - 1) + base for base in bases]
    in_low = [(item >= 0) & (item < width) for item in source]
    in_high = [(item >= -width) & (item < 0) for item in source]
    source = [item & (width - 1) for item in source]
    table = table_ref[...]
    table_sum = jnp.zeros((rows, HEAD_DIM), jnp.float32)
    for head in range(heads):
        part = slice(head * HEAD_DIM, (head + 1) * HEAD_DIM)
        query = query_ref[:, part]
        grad = grad_ref[:, part]
        keys = [key_ref[:, part], near_kv[0, :, part], far_ref[0, :, part]]
        values = [value_ref[:, part], near_kv[1, :, part], far_ref[1, :, part]]
        keys_all = jnp.concatenate(keys + [table], axis=0)
        values_all = jnp.concatenate(values, axis=0)
        content = dot(query, keys_all, NT)
        dprob = dot(grad, values_all, NT)
        relative = [content[:, 3 * width : 4 * width], content[:, 4 * width :]]
        scores = []
        for step in range(3):
            moved = lanes(relative[1], place[step])
            if step > 0:
                moved = jnp.where(upper[step], moved, lanes(relative[0], place[step]))
            score = scale * (content[:, step * width : (step + 1) * width] + moved)
            if step == 0:
                score = jnp.where(seen, score, -jnp.inf)
            else:
                score = score + biases[step - 1]
            scores.append(score)
        dprobs = [dprob[:, step * width : (step + 1) * width] for step in range(3)]
        top = jnp.max(jnp.maximum(jnp.maximum(scores[0], scores[1]), scores[2]), axis=1, keepdims=True)
        exps = [jnp.exp(score - top) for score in scores]
        total = jnp.sum(exps[0] + exps[1] + exps[2], axis=1, keepdims=True)
        mixed = exps[0] * dprobs[0] + exps[1] * dprobs[1] + exps[2] * dprobs[2]
        inverse = 1.0 / total
        delta = jnp.sum(mixed, axis=1, keepdims=True) * inverse
        probs = [e * inverse for e in exps]
        weights = jnp.concatenate([p.astype(jnp.bfloat16) for p in probs], axis=1)
        dscores = [scale * p * (d - delta) for p, d in zip(probs, dprobs)]
        over = jnp.where(high[0], dscores[0], 0.0) + jnp.where(high[1], dscores[1], 0.0)
        over = jnp.sum(over, axis=1, keepdims=True)
        under = jnp.sum(jnp.where(low, dscores[2], 0.0), axis=1, keepdims=True)
        moved = [lanes(item, index) for item, index in zip(dscores, source)]
        below = jnp.where(in_low[1], moved[1], 0.0) + jnp.where(in_low[2], moved[2], 0.0)
        above = jnp.where(in_high[0], moved[0], 0.0) + jnp.where(in_high[1], moved[1], 0.0)
        above = above + jnp.where(in_high[2], moved[2], 0.0)
        below = below + jnp.where(col == 0, under, 0.0)
        above = above + jnp.where(col == width - 1, over, 0.0)
        terms = jnp.concatenate(dscores + [below, above], axis=1).astype(jnp.bfloat16)
        query_out[:, part] = dot(terms, keys_all).astype(query_out.dtype)
        by_key = dot(terms, query, TN)
        by_value = dot(weights, grad, TN)
        own_out[0, :, part] = by_key[:width]
        own_out[1, :, part] = by_value[:width]
        near_out[0, :, part] = by_key[width : 2 * width].astype(jnp.bfloat16)
        near_out[1, :, part] = by_value[width : 2 * width].astype(jnp.bfloat16)
        far_out[0, :, part] = by_key[2 * width : 3 * width].astype(jnp.bfloat16)
        far_out[1, :, part] = by_value[2 * width :].astype(jnp.bfloat16)
        table_sum = table_sum + by_key[3 * width :]
    table_out[...] = table_sum


def block_grads(block, mask, shift, query, grad, key, value, far, pair, cross, table_flipped):
    width, span = query.shape
    vmem = pl.BlockSpec(memory_space=pltpu.VMEM)
    smem = pl.BlockSpec(memory_space=pltpu.SMEM)
    both = (2, width, span)
    return pl.pallas_call(
        block_kernel,
        out_shape=(
            jax.ShapeDtypeStruct((width, span), jnp.bfloat16),
            jax.ShapeDtypeStruct(both, jnp.float32),
            jax.ShapeDtypeStruct(both, jnp.bfloat16),
            jax.ShapeDtypeStruct(both, jnp.bfloat16),
            jax.ShapeDtypeStruct(table_flipped.shape, jnp.float32),
        ),
        in_specs=[smem] * 3 + [vmem] * 8,
        out_specs=(vmem,) * 5,
        scratch_shapes=[pltpu.VMEM(both, jnp.bfloat16)],
        compiler_params=pltpu.CompilerParams(vmem_limit_bytes=32 * 1024 * 1024),
        name="block_grads",
    )(block, mask, shift, query, grad, key, value, far, pair, cross, table_flipped)


def rings(mesh_sizes):
    ctx, head = mesh_sizes
    depth = 32
    columns = ctx // depth
    planes = [
        [
            ((column * depth + z * 2 + core) * head + half)
            for column in range(columns)
            for core in range(2)
            for half in range(head)
        ]
        for z in range(depth // 2)
    ]
    lines = [
        [((column * depth + z * 2 + core) * head + half) for z in range(depth // 2)]
        for column in range(columns)
        for core in range(2)
        for half in range(head)
    ]
    return planes, lines


def table_total(partial, mesh_sizes):
    rows, dim = partial.shape
    planes, lines = rings(mesh_sizes)
    plane, line = len(planes[0]), len(lines[0])
    small = rows // plane
    pieces = lax.all_to_all(
        partial.reshape(plane, small, dim), AXES, 0, 0, axis_index_groups=planes
    )
    piece = jnp.sum(pieces, axis=0)[::-1]
    copies = jnp.broadcast_to(piece[None], (line, small, dim))
    copies = lax.all_to_all(copies, AXES, 0, 0, axis_index_groups=lines)
    piece = jnp.sum(copies, axis=0)
    copies = jnp.broadcast_to(piece[None], (plane, small, dim))
    copies = lax.all_to_all(
        copies, AXES, 0, 0, axis_index_groups=[group[::-1] for group in planes]
    )
    return copies.reshape(rows, dim)


def shards(queries, key_states, value_states, out_grad, rel_table, block_mask, distance_shift):
    count = lax.axis_size("ctx")
    block = lax.axis_index("ctx").astype(jnp.int32).reshape(1)
    pairs = [[i, i + 1] for i in range(0, count, 2)]
    kv = jnp.stack([key_states, value_states])
    far = lax.ppermute(kv, "ctx", [(i, (i + 2) % count) for i in range(count)])
    pair = lax.all_gather(kv, "ctx", axis_index_groups=pairs)
    cross = lax.all_gather(far, "ctx", axis_index_groups=pairs)
    query_grad, own, near_part, far_part, table_part = block_grads(
        block, block_mask, distance_shift, queries, out_grad, key_states, value_states, far, pair,
        cross, rel_table[::-1]
    )
    near_part = lax.ppermute(near_part, "ctx", [(i, (i - 1) % count) for i in range(count)])
    far_part = lax.ppermute(far_part, "ctx", [(i, (i - 2) % count) for i in range(count)])
    table_grad = table_total(table_part, (count, lax.axis_size("head")))
    total = own + near_part.astype(jnp.float32) + far_part.astype(jnp.float32)
    total = total.astype(jnp.bfloat16)
    return query_grad, total[0], total[1], table_grad


def solution(mesh):
    return jax.shard_map(
        shards,
        mesh=mesh,
        in_specs=(
            P("ctx", "head"),
            P("ctx", "head"),
            P("ctx", "head"),
            P("ctx", "head"),
            P(),
            P("ctx", None),
            P("ctx", None),
        ),
        out_specs=(P("ctx", "head"), P("ctx", "head"), P("ctx", "head"), P()),
        check_vma=False,
    )
```

```python
import functools

import jax
import jax.numpy as jnp
from jax import lax
from jax.experimental import pallas as pl
from jax.experimental.pallas import tpu as pltpu
from jax.sharding import PartitionSpec as P

HEAD_DIM = 128
STEPS = 3
AXES = ("ctx", "head")
NN = (((1,), (0,)), ((), ()))
NT = (((1,), (1,)), ((), ()))
TN = (((0,), (0,)), ((), ()))
SCALE = HEAD_DIM ** (-0.5)


def dot(a, b, dims=NN):
    return lax.dot_general(a, b, dims, preferred_element_type=jnp.float32)


def lanes(values, index):
    return jnp.take_along_axis(values, index, axis=1, mode="promise_in_bounds")


def head_parts(span):
    return [slice(at, at + HEAD_DIM) for at in range(0, span, HEAD_DIM)]


def iotas(width):
    row = lax.broadcasted_iota(jnp.int32, (width, width), 0)
    col = lax.broadcasted_iota(jnp.int32, (width, width), 1)
    return row, col


def call(kernel, outs, ins, spaces, scratch, micros, name):
    return pl.pallas_call(
        kernel,
        out_shape=tuple(jax.ShapeDtypeStruct(shape, kind) for shape, kind in outs),
        in_specs=[pl.BlockSpec(memory_space=space) for space in spaces],
        out_specs=(pl.BlockSpec(memory_space=pltpu.VMEM),) * len(outs),
        scratch_shapes=scratch,
        compiler_params=pltpu.CompilerParams(vmem_limit_bytes=32 * 1024 * 1024),
        cost_estimate=pl.CostEstimate(
            flops=micros * 1_000_000_000, bytes_accessed=0, transcendentals=0
        ),
        name=name,
    )(*ins)


def own_kernel(
    block_ref, facts_ref, query_ref, grad_ref, key_ref, value_ref, near_ref, far_ref, table_ref,
    score_out, moved_out, dprob_out, turned_out
):
    width, span = query_ref.shape
    rows = table_ref.shape[0]
    other = 1 - lax.rem(block_ref[0], 2)
    row, col = iotas(width)
    seen = col <= row
    biases = [
        jnp.where(facts_ref[STEPS + step : STEPS + step + 1, :] == 1, 0.0, -jnp.inf)
        for step in range(STEPS)
    ]
    place = [
        jnp.clip(col - row + (rows - 1) - facts_ref[step : step + 1, :], 0, rows - 1)
        for step in range(STEPS)
    ]
    upper = [item >= width for item in place]
    place = [item & (width - 1) for item in place]
    table = table_ref[...]
    for part in head_parts(span):
        query = query_ref[:, part]
        turned_out[part, :] = query.T
        values = [value_ref[:, part], near_ref[other, :, part], far_ref[:, part]]
        dprob = dot(grad_ref[:, part], jnp.concatenate(values, axis=0), NT) * SCALE
        for step in range(STEPS):
            dprob_out[step, :, part] = dprob[:, step * width : (step + 1) * width]
        content = dot(query, jnp.concatenate([key_ref[:, part], table], axis=0), NT) * SCALE
        relative = [content[:, at : at + width] for at in (width, 2 * width)]
        for step in range(STEPS):
            moved = lanes(relative[1], place[step])
            if step == 0:
                score_out[:, part] = jnp.where(seen, content[:, :width] + moved, -jnp.inf)
            else:
                moved = jnp.where(upper[step], moved, lanes(relative[0], place[step]))
                moved_out[step - 1, :, part] = moved + biases[step]


def table_kernel(
    block_ref, facts_ref, query_ref, near_ref, far_ref, score_ref, moved_ref, dprob_ref, turned_ref,
    table_out, terms_out, weight_out
):
    width, span = query_ref.shape
    rows = table_out.shape[0]
    other = 1 - lax.rem(block_ref[0], 2)
    row, col = iotas(width)
    bases = [facts_ref[step : step + 1, :] for step in range(STEPS)]
    place = [col - row + (rows - 1) - base for base in bases]
    high = [place[0] > rows - 1, place[1] > rows - 1]
    low = place[2] < 0
    source = [col + row - (rows - 1) + base for base in bases]
    in_low = [(item >= 0) & (item < width) for item in source]
    in_high = [(item >= -width) & (item < 0) for item in source]
    source = [item & (width - 1) for item in source]
    table_sum = jnp.zeros((HEAD_DIM, rows), jnp.float32)
    for index, part in enumerate(head_parts(span)):
        keys = jnp.concatenate([near_ref[other, :, part], far_ref[:, part]], axis=0)
        content = dot(query_ref[:, part], keys, NT) * SCALE
        scores = [score_ref[:, part]]
        for step in range(1, STEPS):
            scores.append(content[:, (step - 1) * width : step * width] + moved_ref[step - 1, :, part])
        top = jnp.max(jnp.maximum(jnp.maximum(scores[0], scores[1]), scores[2]), axis=1, keepdims=True)
        exps = [jnp.exp(score - top) for score in scores]
        dprobs = [dprob_ref[step, :, part] for step in range(STEPS)]
        total = jnp.sum(exps[0] + exps[1] + exps[2], axis=1, keepdims=True)
        mixed = exps[0] * dprobs[0] + exps[1] * dprobs[1] + exps[2] * dprobs[2]
        mixed = jnp.sum(mixed, axis=1, keepdims=True)
        inverse = 1.0 / total
        delta = mixed * inverse
        probs = [item * inverse for item in exps]
        dscores = [p * (d - delta) for p, d in zip(probs, dprobs)]
        over = jnp.where(high[0], dscores[0], 0.0) + jnp.where(high[1], dscores[1], 0.0)
        over = jnp.sum(over, axis=1, keepdims=True)
        under = jnp.sum(jnp.where(low, dscores[2], 0.0), axis=1, keepdims=True)
        moved = [lanes(item, at) for item, at in zip(dscores, source)]
        below = jnp.where(in_low[1], moved[1], 0.0) + jnp.where(in_low[2], moved[2], 0.0)
        above = jnp.where(in_high[0], moved[0], 0.0) + jnp.where(in_high[1], moved[1], 0.0)
        above = above + jnp.where(in_high[2], moved[2], 0.0)
        below = below + jnp.where(col == 0, under, 0.0)
        above = above + jnp.where(col == width - 1, over, 0.0)
        relative = jnp.concatenate([below, above], axis=1).astype(jnp.bfloat16)
        table_sum = table_sum + dot(turned_ref[part, :], relative)
        for step in range(STEPS):
            at = slice(step * width, (step + 1) * width)
            terms_out[index, :, at] = dscores[step].astype(jnp.bfloat16)
            weight_out[index, :, at] = probs[step].astype(jnp.bfloat16)
        terms_out[index, :, STEPS * width :] = relative
    table_out[...] = table_sum.T


def grads_kernel(
    block_ref, query_ref, grad_ref, key_ref, near_ref, far_ref, table_ref, terms_ref, weight_ref,
    near_out, far_out, query_out, own_out
):
    width, span = query_ref.shape
    other = 1 - lax.rem(block_ref[0], 2)
    table = table_ref[...]
    for index, part in enumerate(head_parts(span)):
        query = query_ref[:, part]
        grad = grad_ref[:, part]
        terms = terms_ref[index]
        keys = [key_ref[:, part], near_ref[other, :, part], far_ref[:, part], table]
        query_out[:, part] = dot(terms, jnp.concatenate(keys, axis=0)).astype(query_out.dtype)
        by_key = dot(terms[:, : STEPS * width], query, TN)
        by_value = dot(weight_ref[index], grad, TN)
        for slot, item in enumerate((by_key, by_value)):
            own_out[slot, :, part] = item[:width]
            near_out[slot, :, part] = item[width : 2 * width].astype(jnp.bfloat16)
            far_out[slot, :, part] = item[2 * width :].astype(jnp.bfloat16)


def spread_kernel(flipped, pieces_ref, copies_out):
    total = pieces_ref[0]
    for index in range(1, pieces_ref.shape[0]):
        total = total + pieces_ref[index]
    if flipped:
        small = total.shape[0]
        total = jnp.concatenate([total[at : at + 1] for at in reversed(range(small))], axis=0)
    for index in range(copies_out.shape[0]):
        copies_out[index] = total


def rings(count, head):
    depth = 32
    columns = count // depth
    planes = [
        [
            (column * depth + z * 2 + core) * head + half
            for column in range(columns)
            for core in range(2)
            for half in range(head)
        ]
        for z in range(depth // 2)
    ]
    lines = [
        [(column * depth + z * 2 + core) * head + half for z in range(depth // 2)]
        for column in range(columns)
        for core in range(2)
        for half in range(head)
    ]
    return planes, lines


def shards(queries, key_states, value_states, out_grad, rel_table, block_mask, distance_shift):
    count = lax.axis_size("ctx")
    width, span = queries.shape
    rows = rel_table.shape[0]
    heads = span // HEAD_DIM
    block = lax.axis_index("ctx").astype(jnp.int32).reshape(1)
    odd = lax.rem(block[0], 2) == 1
    pairs = [[i, i + 1] for i in range(0, count, 2)]
    ahead = [(i, (i + 2) % count) for i in range(count)]
    one, two, three = (width, span), (2, width, span), (STEPS, width, span)
    bf, f32 = jnp.bfloat16, jnp.float32
    scalar, local = [pltpu.SMEM], [pltpu.VMEM]
    step = jnp.arange(STEPS, dtype=jnp.int32)
    visible = (block_mask[0] == 1) & (block[0] >= step)
    facts = [step * width - distance_shift[0], visible.astype(jnp.int32), step[:2]]
    facts = jnp.broadcast_to(jnp.concatenate(facts)[:, None], (8, width))
    table = rel_table[::-1]
    far_key = lax.ppermute(key_states, "ctx", ahead)
    far_value = lax.ppermute(value_states, "ctx", ahead)
    near_value = lax.all_gather(jnp.where(odd, far_value, value_states), "ctx", axis_index_groups=pairs)
    score, moved, dprob, turned = call(
        own_kernel,
        ((one, f32), (two, f32), (three, f32), ((span, width), bf)),
        (block, facts, queries, out_grad, key_states, value_states, near_value, far_value, table),
        scalar + local * 8, [], 3, "own_scores",
    )
    far_key, score = lax.optimization_barrier((far_key, score))
    near_key = lax.all_gather(jnp.where(odd, far_key, key_states), "ctx", axis_index_groups=pairs)
    table_part, terms, weight = call(
        table_kernel,
        (
            ((rows, HEAD_DIM), f32), ((heads, width, STEPS * width + rows), bf),
            ((heads, width, STEPS * width), bf),
        ),
        (block, facts, queries, near_key, far_key, score, moved, dprob, turned),
        scalar + local * 8, [], 4, "table_part",
    )
    near_part, far_part, query_grad, own = call(
        grads_kernel,
        ((two, bf), (two, bf), (one, bf), (two, f32)),
        (block, queries, out_grad, key_states, near_key, far_key, table, terms, weight),
        scalar + local * 8, [], 4, "block_grads",
    )
    planes, lines = rings(count, lax.axis_size("head"))
    small = rows // len(planes[0])
    shape = (len(planes[0]), small, HEAD_DIM)
    table_part, near_part, far_part = lax.optimization_barrier((table_part, near_part, far_part))
    near_part = lax.ppermute(near_part, "ctx", [(i, (i - 1) % count) for i in range(count)])
    far_part = lax.ppermute(far_part, "ctx", [(i, (i - 2) % count) for i in range(count)])
    pieces = lax.all_to_all(table_part.reshape(shape), AXES, 0, 0, axis_index_groups=planes)
    (copies,) = call(
        functools.partial(spread_kernel, True),
        (((len(lines[0]), small, HEAD_DIM), f32),), (pieces,), local, [], 40, "plane_sum",
    )
    pieces = lax.all_to_all(copies, AXES, 0, 0, axis_index_groups=lines)
    (copies,) = call(
        functools.partial(spread_kernel, False), ((shape, f32),), (pieces,), local, [], 1, "line_sum",
    )
    copies = lax.all_to_all(copies, AXES, 0, 0, axis_index_groups=[plane[::-1] for plane in planes])
    table_grad = copies.reshape(rows, HEAD_DIM)
    total = own + near_part.astype(f32) + far_part.astype(f32)
    total = total.astype(bf)
    return query_grad, total[0], total[1], table_grad


def solution(mesh):
    return jax.shard_map(
        shards,
        mesh=mesh,
        in_specs=(
            P("ctx", "head"),
            P("ctx", "head"),
            P("ctx", "head"),
            P("ctx", "head"),
            P(),
            P("ctx", None),
            P("ctx", None),
        ),
        out_specs=(P("ctx", "head"), P("ctx", "head"), P("ctx", "head"), P()),
        check_vma=False,
    )
```

```python
import functools

import jax
import jax.numpy as jnp
from jax import lax
from jax.experimental import pallas as pl
from jax.experimental.pallas import tpu as pltpu
from jax.sharding import PartitionSpec as P

HEAD_DIM = 128
STEPS = 3
AXES = ("ctx", "head")
NN = (((1,), (0,)), ((), ()))
NT = (((1,), (1,)), ((), ()))
TN = (((0,), (0,)), ((), ()))
SCALE = HEAD_DIM ** (-0.5)


def dot(a, b, dims=NN):
    return lax.dot_general(a, b, dims, preferred_element_type=jnp.float32)


def lanes(values, index):
    return jnp.take_along_axis(values, index, axis=1, mode="promise_in_bounds")


def head_parts(span):
    return [slice(at, at + HEAD_DIM) for at in range(0, span, HEAD_DIM)]


def iotas(width):
    row = lax.broadcasted_iota(jnp.int32, (width, width), 0)
    col = lax.broadcasted_iota(jnp.int32, (width, width), 1)
    return row, col


def call(kernel, outs, ins, spaces, scratch, micros, name):
    return pl.pallas_call(
        kernel,
        out_shape=tuple(jax.ShapeDtypeStruct(shape, kind) for shape, kind in outs),
        in_specs=[pl.BlockSpec(memory_space=space) for space in spaces],
        out_specs=(pl.BlockSpec(memory_space=pltpu.VMEM),) * len(outs),
        scratch_shapes=scratch,
        compiler_params=pltpu.CompilerParams(vmem_limit_bytes=32 * 1024 * 1024),
        cost_estimate=pl.CostEstimate(
            flops=micros * 1_000_000_000, bytes_accessed=0, transcendentals=0
        ),
        name=name,
    )(*ins)


def flip_kernel(flip_out):
    row, col = iotas(flip_out.shape[0])
    last = flip_out.shape[0] - 1
    flip_out[...] = jnp.where(row + col == last, 1.0, 0.0).astype(flip_out.dtype)


def own_kernel(
    block_ref, mask_ref, shift_ref, query_ref, grad_ref, key_ref, value_ref, table_ref, flip_ref,
    score_out, moved_out, dprob_out, turned_out, facts_out, table_out
):
    width, span = query_ref.shape
    rows = table_ref.shape[0]
    row, col = iotas(width)
    seen = col <= row
    bases = [step * width - shift_ref[0, step] for step in range(STEPS)]
    biases = [
        jnp.where((mask_ref[0, step] == 1) & (block_ref[0] >= step), 0.0, -jnp.inf)
        for step in range(STEPS)
    ]
    line = lax.broadcasted_iota(jnp.int32, facts_out.shape, 0)
    facts = jnp.zeros(facts_out.shape, jnp.int32)
    for step in range(STEPS):
        facts = jnp.where(line == step, bases[step], facts)
    facts_out[...] = facts
    place = [jnp.clip(col - row + (rows - 1) - base, 0, rows - 1) for base in bases]
    upper = [item >= width for item in place]
    place = [item & (width - 1) for item in place]
    table = dot(flip_ref[...], table_ref[...]).astype(jnp.bfloat16)
    table_out[...] = table
    for part in head_parts(span):
        query = query_ref[:, part]
        turned_out[part, :] = query.T
        dprob_out[:, part] = dot(grad_ref[:, part], value_ref[:, part], NT) * SCALE
        content = dot(query, jnp.concatenate([key_ref[:, part], table], axis=0), NT) * SCALE
        relative = [content[:, at : at + width] for at in (width, 2 * width)]
        for step in range(STEPS):
            moved = lanes(relative[1], place[step])
            if step == 0:
                score_out[:, part] = jnp.where(seen, content[:, :width] + moved, -jnp.inf)
            else:
                moved = jnp.where(upper[step], moved, lanes(relative[0], place[step]))
                moved_out[step - 1, :, part] = moved + biases[step]


def table_kernel(
    block_ref, facts_ref, query_ref, grad_ref, near_key_ref, near_value_ref, far_key_ref, far_value_ref,
    score_ref, moved_ref, dprob_ref, turned_ref, table_out, terms_out, weight_out
):
    width, span = query_ref.shape
    rows = table_out.shape[0]
    parts = head_parts(span)
    group = 3 if len(parts) % 3 == 0 else 1
    other = 1 - lax.rem(block_ref[0], 2)
    row, col = iotas(width)
    bases = [facts_ref[step : step + 1, :] for step in range(STEPS)]
    place = [col - row + (rows - 1) - base for base in bases]
    clamps = [place[0] > rows - 1, place[1] > rows - 1, place[2] < 0]
    source = [col + row - (rows - 1) + base for base in bases]
    in_low = [(item >= 0) & (item < width) for item in source]
    in_high = [(item >= -width) & (item < 0) for item in source]
    source = [item & (width - 1) for item in source]
    item_row = lax.broadcasted_iota(jnp.int32, (STEPS * width, rows), 0)
    item_col = lax.broadcasted_iota(jnp.int32, (STEPS * width, rows), 1)
    ends = item_col == jnp.where(item_row < 2 * width, rows - 1, 0)
    ends = jnp.where(ends, 1.0, 0.0).astype(jnp.bfloat16)
    table_sum = jnp.zeros((HEAD_DIM, rows), jnp.float32)

    def many(item):
        return jnp.concatenate([item] * group, axis=0)

    for start in range(0, len(parts), group):
        mine = parts[start : start + group]

        def heads(load):
            return jnp.concatenate([load(part) for part in mine], axis=0)

        def products(left_ref, near_ref, far_ref):
            return heads(
                lambda part: dot(
                    left_ref[:, part],
                    jnp.concatenate([near_ref[other, :, part], far_ref[:, part]], axis=0),
                    NT,
                )
            ) * SCALE

        content = products(query_ref, near_key_ref, far_key_ref)
        dprob = products(grad_ref, near_value_ref, far_value_ref)
        scores = [heads(lambda part: score_ref[:, part])]
        dprobs = [heads(lambda part: dprob_ref[:, part])]
        for step in range(1, STEPS):
            at = slice((step - 1) * width, step * width)
            scores.append(content[:, at] + heads(lambda part: moved_ref[step - 1, :, part]))
            dprobs.append(dprob[:, at])
        top = jnp.maximum(jnp.maximum(scores[0], scores[1]), scores[2])
        top = jnp.max(top, axis=1, keepdims=True)
        exps = [jnp.exp(score - top) for score in scores]
        total = jnp.sum(exps[0] + exps[1] + exps[2], axis=1, keepdims=True)
        mixed = exps[0] * dprobs[0] + exps[1] * dprobs[1] + exps[2] * dprobs[2]
        mixed = jnp.sum(mixed, axis=1, keepdims=True)
        inverse = 1.0 / total
        delta = mixed * inverse
        probs = [item * inverse for item in exps]
        dscores = [p * (d - delta) for p, d in zip(probs, dprobs)]
        rounded = [item.astype(jnp.bfloat16) for item in dscores]
        moved = [lanes(item, many(at)) for item, at in zip(dscores, source)]
        below = jnp.where(many(in_low[1]), moved[1], 0.0) + jnp.where(many(in_low[2]), moved[2], 0.0)
        above = jnp.where(many(in_high[0]), moved[0], 0.0) + jnp.where(many(in_high[1]), moved[1], 0.0)
        above = above + jnp.where(many(in_high[2]), moved[2], 0.0)
        clamped = [
            jnp.where(many(mask), item, 0.0).astype(jnp.bfloat16)
            for mask, item in zip(clamps, dscores)
        ]
        clamped = dot(jnp.concatenate(clamped, axis=1), ends)
        relative = (jnp.concatenate([below, above], axis=1) + clamped).astype(jnp.bfloat16)
        for at, part in enumerate(mine):
            here = slice(at * width, (at + 1) * width)
            table_sum = table_sum + dot(turned_ref[part, :], relative[here])
            for step in range(STEPS):
                to = slice(step * width, (step + 1) * width)
                terms_out[start + at, :, to] = rounded[step][here]
                weight_out[start + at, :, to] = probs[step][here].astype(jnp.bfloat16)
            terms_out[start + at, :, STEPS * width :] = relative[here]
    table_out[...] = table_sum.T


def grads_kernel(
    block_ref, query_ref, grad_ref, key_ref, near_ref, far_ref, table_ref, terms_ref, weight_ref,
    near_out, far_out, query_out, own_out
):
    width, span = query_ref.shape
    other = 1 - lax.rem(block_ref[0], 2)
    table = table_ref[...]
    for index, part in enumerate(head_parts(span)):
        query = query_ref[:, part]
        grad = grad_ref[:, part]
        terms = terms_ref[index]
        keys = [key_ref[:, part], near_ref[other, :, part], far_ref[:, part], table]
        query_out[:, part] = dot(terms, jnp.concatenate(keys, axis=0)).astype(query_out.dtype)
        by_key = dot(terms[:, : STEPS * width], query, TN)
        by_value = dot(weight_ref[index], grad, TN)
        for slot, item in enumerate((by_key, by_value)):
            own_out[slot, :, part] = item[:width]
            near_out[slot, :, part] = item[width : 2 * width].astype(jnp.bfloat16)
            far_out[slot, :, part] = item[2 * width :].astype(jnp.bfloat16)


def spread_kernel(flipped, pieces_ref, copies_out):
    total = pieces_ref[0]
    for index in range(1, pieces_ref.shape[0]):
        total = total + pieces_ref[index]
    if flipped:
        small = total.shape[0]
        total = jnp.concatenate([total[at : at + 1] for at in reversed(range(small))], axis=0)
    for index in range(copies_out.shape[0]):
        copies_out[index] = total


def rings(count, head):
    depth = 16
    columns = count // (2 * depth)
    lead = 9
    planes = []
    for z in range(depth):
        plane = [
            (column * 2 * depth + z * 2 + core) * head + half
            for column in range(columns)
            for core in range(2)
            for half in range(head)
        ]
        far = plane.pop(len(plane) * 9 // 32)
        planes.append(plane + [far])
    lines = [
        [
            (column * 2 * depth + (z + lead) % depth * 2 + core) * head + half
            for z in range(depth)
        ]
        for column in range(columns)
        for core in range(2)
        for half in range(head)
    ]
    return planes, lines


def shards(queries, key_states, value_states, out_grad, rel_table, block_mask, distance_shift):
    count = lax.axis_size("ctx")
    width, span = queries.shape
    rows = rel_table.shape[0]
    heads = span // HEAD_DIM
    block = lax.axis_index("ctx").astype(jnp.int32).reshape(1)
    odd = lax.rem(block[0], 2) == 1
    pairs = [[i, i + 1] for i in range(0, count, 2)]
    ahead = [(i, (i + 2) % count) for i in range(count)]
    one, two, three = (width, span), (2, width, span), (STEPS, width, span)
    bf, f32 = jnp.bfloat16, jnp.float32
    scalar, local = [pltpu.SMEM], [pltpu.VMEM]
    far_value = lax.ppermute(value_states, "ctx", ahead)
    far_key = lax.ppermute(key_states, "ctx", ahead)
    (flip,) = call(flip_kernel, (((rows, rows), bf),), (), [], [], 10, "flip")
    score, moved, dprob, turned, facts, table = call(
        own_kernel,
        (
            (one, f32), (two, f32), (one, f32), ((span, width), bf), ((8, width), jnp.int32),
            (rel_table.shape, bf),
        ),
        (
            block, block_mask, distance_shift, queries, out_grad, key_states, value_states,
            rel_table, flip,
        ),
        scalar * 3 + local * 6, [], 3, "own_scores",
    )
    far_value, score = lax.optimization_barrier((far_value, score))
    near_value = lax.all_gather(jnp.where(odd, far_value, value_states), "ctx", axis_index_groups=pairs)
    far_key, near_value = lax.optimization_barrier((far_key, near_value))
    near_key = lax.all_gather(jnp.where(odd, far_key, key_states), "ctx", axis_index_groups=pairs)
    table_part, terms, weight = call(
        table_kernel,
        (
            ((rows, HEAD_DIM), f32), ((heads, width, STEPS * width + rows), bf),
            ((heads, width, STEPS * width), bf),
        ),
        (
            block, facts, queries, out_grad, near_key, near_value, far_key, far_value,
            score, moved, dprob, turned,
        ),
        scalar + local * 11, [], 4, "table_part",
    )
    near_part, far_part, query_grad, own = call(
        grads_kernel,
        ((two, bf), (two, bf), (one, bf), (two, f32)),
        (block, queries, out_grad, key_states, near_key, far_key, table, terms, weight),
        scalar + local * 8, [], 4, "block_grads",
    )
    planes, lines = rings(count, lax.axis_size("head"))
    small = rows // len(planes[0])
    shape = (len(planes[0]), small, HEAD_DIM)
    table_part, near_part, far_part = lax.optimization_barrier((table_part, near_part, far_part))
    near_part = lax.ppermute(near_part, "ctx", [(i, (i - 1) % count) for i in range(count)])
    far_part = lax.ppermute(far_part, "ctx", [(i, (i - 2) % count) for i in range(count)])
    pieces = lax.all_to_all(table_part.reshape(shape), AXES, 0, 0, axis_index_groups=planes)
    (copies,) = call(
        functools.partial(spread_kernel, True),
        (((len(lines[0]), small, HEAD_DIM), f32),), (pieces,), local, [], 40, "plane_sum",
    )
    pieces = lax.all_to_all(copies, AXES, 0, 0, axis_index_groups=lines)
    (copies,) = call(
        functools.partial(spread_kernel, False), ((shape, f32),), (pieces,), local, [], 1, "line_sum",
    )
    copies = lax.all_to_all(copies, AXES, 0, 0, axis_index_groups=[plane[::-1] for plane in planes])
    table_grad = copies.reshape(rows, HEAD_DIM)
    total = own + near_part.astype(f32) + far_part.astype(f32)
    total = total.astype(bf)
    return query_grad, total[0], total[1], table_grad


def solution(mesh):
    return jax.shard_map(
        shards,
        mesh=mesh,
        in_specs=(
            P("ctx", "head"),
            P("ctx", "head"),
            P("ctx", "head"),
            P("ctx", "head"),
            P(),
            P("ctx", None),
            P("ctx", None),
        ),
        out_specs=(P("ctx", "head"), P("ctx", "head"), P("ctx", "head"), P()),
        check_vma=False,
    )
```

```python
import functools

import jax
import jax.numpy as jnp
from jax import lax
from jax.experimental import pallas as pl
from jax.experimental.pallas import tpu as pltpu
from jax.sharding import PartitionSpec as P

HEAD_DIM = 128
STEPS = 3
AXES = ("ctx", "head")
NN = (((1,), (0,)), ((), ()))
NT = (((1,), (1,)), ((), ()))
TN = (((0,), (0,)), ((), ()))
SCALE = HEAD_DIM ** (-0.5)


def dot(a, b, dims=NN):
    return lax.dot_general(a, b, dims, preferred_element_type=jnp.float32)


def lanes(values, index):
    return jnp.take_along_axis(values, index, axis=1, mode="promise_in_bounds")


def head_parts(span):
    return [slice(at, at + HEAD_DIM) for at in range(0, span, HEAD_DIM)]


def iotas(width):
    row = lax.broadcasted_iota(jnp.int32, (width, width), 0)
    col = lax.broadcasted_iota(jnp.int32, (width, width), 1)
    return row, col


def call(kernel, outs, ins, spaces, scratch, micros, name):
    return pl.pallas_call(
        kernel,
        out_shape=tuple(jax.ShapeDtypeStruct(shape, kind) for shape, kind in outs),
        in_specs=[pl.BlockSpec(memory_space=space) for space in spaces],
        out_specs=(pl.BlockSpec(memory_space=pltpu.VMEM),) * len(outs),
        scratch_shapes=scratch,
        compiler_params=pltpu.CompilerParams(vmem_limit_bytes=32 * 1024 * 1024),
        cost_estimate=pl.CostEstimate(
            flops=micros * 1_000_000_000, bytes_accessed=0, transcendentals=0
        ),
        name=name,
    )(*ins)


def flip_kernel(flip_out):
    row, col = iotas(flip_out.shape[0])
    last = flip_out.shape[0] - 1
    flip_out[...] = jnp.where(row + col == last, 1.0, 0.0).astype(flip_out.dtype)


def own_kernel(
    block_ref, mask_ref, shift_ref, query_ref, grad_ref, key_ref, value_ref, table_ref, flip_ref,
    score_out, moved_out, dprob_out, turned_out, facts_out, table_out
):
    width, span = query_ref.shape
    rows = table_ref.shape[0]
    row, col = iotas(width)
    seen = col <= row
    bases = [step * width - shift_ref[0, step] for step in range(STEPS)]
    biases = [
        jnp.where((mask_ref[0, step] == 1) & (block_ref[0] >= step), 0.0, -jnp.inf)
        for step in range(STEPS)
    ]
    line = lax.broadcasted_iota(jnp.int32, facts_out.shape, 0)
    facts = jnp.zeros(facts_out.shape, jnp.int32)
    for step in range(STEPS):
        facts = jnp.where(line == step, bases[step], facts)
    facts_out[...] = facts
    place = [jnp.clip(col - row + (rows - 1) - base, 0, rows - 1) for base in bases]
    upper = [item >= width for item in place]
    place = [item & (width - 1) for item in place]
    table = dot(flip_ref[...], table_ref[...]).astype(jnp.bfloat16)
    table_out[...] = table
    for part in head_parts(span):
        query = query_ref[:, part]
        turned_out[part, :] = query.T
        dprob_out[:, part] = dot(grad_ref[:, part], value_ref[:, part], NT) * SCALE
        content = dot(query, jnp.concatenate([key_ref[:, part], table], axis=0), NT) * SCALE
        relative = [content[:, at : at + width] for at in (width, 2 * width)]
        for step in range(STEPS):
            moved = lanes(relative[1], place[step])
            if step == 0:
                score_out[:, part] = jnp.where(seen, content[:, :width] + moved, -jnp.inf)
            else:
                moved = jnp.where(upper[step], moved, lanes(relative[0], place[step]))
                moved_out[step - 1, :, part] = moved + biases[step]


def table_kernel(
    block_ref, facts_ref, query_ref, grad_ref, near_key_ref, near_value_ref, far_key_ref, far_value_ref,
    score_ref, moved_ref, dprob_ref, turned_ref, table_out, terms_out, weight_out
):
    width, span = query_ref.shape
    rows = table_out.shape[0]
    parts = head_parts(span)
    group = 3 if len(parts) % 3 == 0 else 1
    other = 1 - lax.rem(block_ref[0], 2)
    row, col = iotas(width)
    bases = [facts_ref[step : step + 1, :] for step in range(STEPS)]
    place = [col - row + (rows - 1) - base for base in bases]
    clamps = [place[0] > rows - 1, place[1] > rows - 1, place[2] < 0]
    source = [col + row - (rows - 1) + base for base in bases]
    in_low = [(item >= 0) & (item < width) for item in source]
    in_high = [(item >= -width) & (item < 0) for item in source]
    source = [item & (width - 1) for item in source]
    item_row = lax.broadcasted_iota(jnp.int32, (STEPS * width, rows), 0)
    item_col = lax.broadcasted_iota(jnp.int32, (STEPS * width, rows), 1)
    ends = item_col == jnp.where(item_row < 2 * width, rows - 1, 0)
    ends = jnp.where(ends, 1.0, 0.0).astype(jnp.bfloat16)
    table_sum = jnp.zeros((HEAD_DIM, rows), jnp.float32)

    def many(item):
        return jnp.concatenate([item] * group, axis=0)

    for start in range(0, len(parts), group):
        mine = parts[start : start + group]

        def heads(load):
            return jnp.concatenate([load(part) for part in mine], axis=0)

        def products(left_ref, near_ref, far_ref):
            return heads(
                lambda part: dot(
                    left_ref[:, part],
                    jnp.concatenate([near_ref[other, :, part], far_ref[:, part]], axis=0),
                    NT,
                )
            ) * SCALE

        content = products(query_ref, near_key_ref, far_key_ref)
        dprob = products(grad_ref, near_value_ref, far_value_ref)
        scores = [heads(lambda part: score_ref[:, part])]
        dprobs = [heads(lambda part: dprob_ref[:, part])]
        for step in range(1, STEPS):
            at = slice((step - 1) * width, step * width)
            scores.append(content[:, at] + heads(lambda part: moved_ref[step - 1, :, part]))
            dprobs.append(dprob[:, at])
        top = jnp.maximum(jnp.maximum(scores[0], scores[1]), scores[2])
        top = jnp.max(top, axis=1, keepdims=True)
        exps = [jnp.exp(score - top) for score in scores]
        total = jnp.sum(exps[0] + exps[1] + exps[2], axis=1, keepdims=True)
        mixed = exps[0] * dprobs[0] + exps[1] * dprobs[1] + exps[2] * dprobs[2]
        mixed = jnp.sum(mixed, axis=1, keepdims=True)
        inverse = 1.0 / total
        delta = mixed * inverse
        probs = [item * inverse for item in exps]
        dscores = [p * (d - delta) for p, d in zip(probs, dprobs)]
        rounded = [item.astype(jnp.bfloat16) for item in dscores]
        moved = [lanes(item, many(at)) for item, at in zip(dscores, source)]
        below = jnp.where(many(in_low[1]), moved[1], 0.0) + jnp.where(many(in_low[2]), moved[2], 0.0)
        above = jnp.where(many(in_high[0]), moved[0], 0.0) + jnp.where(many(in_high[1]), moved[1], 0.0)
        above = above + jnp.where(many(in_high[2]), moved[2], 0.0)
        clamped = [
            jnp.where(many(mask), item, 0.0).astype(jnp.bfloat16)
            for mask, item in zip(clamps, dscores)
        ]
        clamped = dot(jnp.concatenate(clamped, axis=1), ends)
        relative = (jnp.concatenate([below, above], axis=1) + clamped).astype(jnp.bfloat16)
        for at, part in enumerate(mine):
            here = slice(at * width, (at + 1) * width)
            table_sum = table_sum + dot(turned_ref[part, :], relative[here])
            for step in range(STEPS):
                to = slice(step * width, (step + 1) * width)
                terms_out[start + at, :, to] = rounded[step][here]
                weight_out[start + at, :, to] = probs[step][here].astype(jnp.bfloat16)
            terms_out[start + at, :, STEPS * width :] = relative[here]
    table_out[...] = table_sum.T


def grads_kernel(
    block_ref, query_ref, grad_ref, key_ref, near_ref, far_ref, table_ref, terms_ref, weight_ref,
    near_out, far_out, query_out, own_out
):
    width, span = query_ref.shape
    other = 1 - lax.rem(block_ref[0], 2)
    table = table_ref[...]
    for index, part in enumerate(head_parts(span)):
        query = query_ref[:, part]
        grad = grad_ref[:, part]
        terms = terms_ref[index]
        keys = [key_ref[:, part], near_ref[other, :, part], far_ref[:, part], table]
        query_out[:, part] = dot(terms, jnp.concatenate(keys, axis=0)).astype(query_out.dtype)
        by_key = dot(terms[:, : STEPS * width], query, TN)
        by_value = dot(weight_ref[index], grad, TN)
        for slot, item in enumerate((by_key, by_value)):
            own_out[slot, :, part] = item[:width]
            near_out[slot, :, part] = item[width : 2 * width].astype(jnp.bfloat16)
            far_out[slot, :, part] = item[2 * width :].astype(jnp.bfloat16)


def spread_kernel(flipped, pieces_ref, copies_out):
    total = pieces_ref[0]
    for index in range(1, pieces_ref.shape[0]):
        total = total + pieces_ref[index]
    if flipped:
        small = total.shape[0]
        total = jnp.concatenate([total[at : at + 1] for at in reversed(range(small))], axis=0)
    for index in range(copies_out.shape[0]):
        copies_out[index] = total


def final_kernel(own_ref, near_ref, far_ref, table_ref, key_out, value_out, table_out):
    for slot, out in enumerate((key_out, value_out)):
        total = own_ref[slot] + near_ref[slot].astype(jnp.float32) + far_ref[slot].astype(jnp.float32)
        out[...] = total.astype(out.dtype)
    table_out[...] = table_ref[...]


def rings(count, head):
    depth = 16
    columns = count // (2 * depth)
    lead = 9
    planes = []
    for z in range(depth):
        plane = [
            (column * 2 * depth + z * 2 + core) * head + half
            for column in range(columns)
            for core in range(2)
            for half in range(head)
        ]
        far = plane.pop(len(plane) * 9 // 32)
        planes.append(plane + [far])
    lines = [
        [
            (column * 2 * depth + (z + lead) % depth * 2 + core) * head + half
            for z in range(depth)
        ]
        for column in range(columns)
        for core in range(2)
        for half in range(head)
    ]
    return planes, lines


def shards(queries, key_states, value_states, out_grad, rel_table, block_mask, distance_shift):
    count = lax.axis_size("ctx")
    width, span = queries.shape
    rows = rel_table.shape[0]
    heads = span // HEAD_DIM
    block = lax.axis_index("ctx").astype(jnp.int32).reshape(1)
    odd = lax.rem(block[0], 2) == 1
    pairs = [[i, i + 1] for i in range(0, count, 2)]
    ahead = [(i, (i + 2) % count) for i in range(count)]
    one, two, three = (width, span), (2, width, span), (STEPS, width, span)
    bf, f32 = jnp.bfloat16, jnp.float32
    scalar, local = [pltpu.SMEM], [pltpu.VMEM]
    far_value = lax.ppermute(value_states, "ctx", ahead)
    far_key = lax.ppermute(key_states, "ctx", ahead)
    (flip,) = call(flip_kernel, (((rows, rows), bf),), (), [], [], 10, "flip")
    score, moved, dprob, turned, facts, table = call(
        own_kernel,
        (
            (one, f32), (two, f32), (one, f32), ((span, width), bf), ((8, width), jnp.int32),
            (rel_table.shape, bf),
        ),
        (
            block, block_mask, distance_shift, queries, out_grad, key_states, value_states,
            rel_table, flip,
        ),
        scalar * 3 + local * 6, [], 3, "own_scores",
    )
    far_value, score = lax.optimization_barrier((far_value, score))
    near_value = lax.all_gather(jnp.where(odd, far_value, value_states), "ctx", axis_index_groups=pairs)
    far_key, near_value = lax.optimization_barrier((far_key, near_value))
    near_key = lax.all_gather(jnp.where(odd, far_key, key_states), "ctx", axis_index_groups=pairs)
    table_part, terms, weight = call(
        table_kernel,
        (
            ((rows, HEAD_DIM), f32), ((heads, width, STEPS * width + rows), bf),
            ((heads, width, STEPS * width), bf),
        ),
        (
            block, facts, queries, out_grad, near_key, near_value, far_key, far_value,
            score, moved, dprob, turned,
        ),
        scalar + local * 11, [], 4, "table_part",
    )
    near_part, far_part, query_grad, own = call(
        grads_kernel,
        ((two, bf), (two, bf), (one, bf), (two, f32)),
        (block, queries, out_grad, key_states, near_key, far_key, table, terms, weight),
        scalar + local * 8, [], 4, "block_grads",
    )
    planes, lines = rings(count, lax.axis_size("head"))
    small = rows // len(planes[0])
    shape = (len(planes[0]), small, HEAD_DIM)
    table_part, near_part, far_part = lax.optimization_barrier((table_part, near_part, far_part))
    near_part = lax.ppermute(near_part, "ctx", [(i, (i - 1) % count) for i in range(count)])
    pieces = lax.all_to_all(table_part.reshape(shape), AXES, 0, 0, axis_index_groups=planes)
    (copies,) = call(
        functools.partial(spread_kernel, True),
        (((len(lines[0]), small, HEAD_DIM), f32),), (pieces,), local, [], 40, "plane_sum",
    )
    copies, far_part = lax.optimization_barrier((copies, far_part))
    far_part = lax.ppermute(far_part, "ctx", [(i, (i - 2) % count) for i in range(count)])
    pieces = lax.all_to_all(copies, AXES, 0, 0, axis_index_groups=lines)
    (copies,) = call(
        functools.partial(spread_kernel, False), ((shape, f32),), (pieces,), local, [], 4, "line_sum",
    )
    copies = lax.all_to_all(copies, AXES, 0, 0, axis_index_groups=[plane[::-1] for plane in planes])
    key_grad, value_grad, table_grad = call(
        final_kernel,
        ((one, bf), (one, bf), ((rows, HEAD_DIM), f32)),
        (own, near_part, far_part, copies.reshape(rows, HEAD_DIM)),
        local * 4, [], 1, "final_sums",
    )
    return query_grad, key_grad, value_grad, table_grad


def solution(mesh):
    return jax.shard_map(
        shards,
        mesh=mesh,
        in_specs=(
            P("ctx", "head"),
            P("ctx", "head"),
            P("ctx", "head"),
            P("ctx", "head"),
            P(),
            P("ctx", None),
            P("ctx", None),
        ),
        out_specs=(P("ctx", "head"), P("ctx", "head"), P("ctx", "head"), P()),
        check_vma=False,
    )
```

```python
import functools

import jax
import jax.numpy as jnp
from jax import lax
from jax.experimental import pallas as pl
from jax.experimental.pallas import tpu as pltpu
from jax.sharding import PartitionSpec as P

HEAD_DIM = 128
STEPS = 3
AXES = ("ctx", "head")
NN = (((1,), (0,)), ((), ()))
NT = (((1,), (1,)), ((), ()))
TN = (((0,), (0,)), ((), ()))
SCALE = HEAD_DIM ** (-0.5)


def dot(a, b, dims=NN):
    return lax.dot_general(a, b, dims, preferred_element_type=jnp.float32)


def lanes(values, index):
    return jnp.take_along_axis(values, index, axis=1, mode="promise_in_bounds")


def head_parts(span):
    return [slice(at, at + HEAD_DIM) for at in range(0, span, HEAD_DIM)]


def iotas(width):
    row = lax.broadcasted_iota(jnp.int32, (width, width), 0)
    col = lax.broadcasted_iota(jnp.int32, (width, width), 1)
    return row, col


def call(kernel, outs, ins, spaces, scratch, micros, name):
    return pl.pallas_call(
        kernel,
        out_shape=tuple(jax.ShapeDtypeStruct(shape, kind) for shape, kind in outs),
        in_specs=[pl.BlockSpec(memory_space=space) for space in spaces],
        out_specs=(pl.BlockSpec(memory_space=pltpu.VMEM),) * len(outs),
        scratch_shapes=scratch,
        compiler_params=pltpu.CompilerParams(vmem_limit_bytes=32 * 1024 * 1024),
        cost_estimate=pl.CostEstimate(
            flops=micros * 1_000_000_000, bytes_accessed=0, transcendentals=0
        ),
        name=name,
    )(*ins)


def flip_kernel(flip_out):
    row, col = iotas(flip_out.shape[0])
    last = flip_out.shape[0] - 1
    flip_out[...] = jnp.where(row + col == last, 1.0, 0.0).astype(flip_out.dtype)


def own_kernel(
    block_ref, mask_ref, shift_ref, query_ref, grad_ref, key_ref, value_ref, table_ref, flip_ref,
    score_out, moved_out, dprob_out, turned_out, facts_out, table_out, key_out, value_out
):
    width, span = query_ref.shape
    rows = table_ref.shape[0]
    row, col = iotas(width)
    seen = col <= row
    bases = [step * width - shift_ref[0, step] for step in range(STEPS)]
    biases = [
        jnp.where((mask_ref[0, step] == 1) & (block_ref[0] >= step), 0.0, -jnp.inf)
        for step in range(STEPS)
    ]
    line = lax.broadcasted_iota(jnp.int32, facts_out.shape, 0)
    facts = jnp.zeros(facts_out.shape, jnp.int32)
    for step in range(STEPS):
        facts = jnp.where(line == step, bases[step], facts)
    facts_out[...] = facts
    place = [jnp.clip(col - row + (rows - 1) - base, 0, rows - 1) for base in bases]
    upper = [item >= width for item in place]
    place = [item & (width - 1) for item in place]
    table = dot(flip_ref[...], table_ref[...]).astype(jnp.bfloat16)
    table_out[...] = table
    key_out[...] = key_ref[...]
    value_out[...] = value_ref[...]
    for part in head_parts(span):
        query = query_ref[:, part]
        turned_out[part, :] = query.T
        dprob_out[:, part] = dot(grad_ref[:, part], value_ref[:, part], NT) * SCALE
        content = dot(query, jnp.concatenate([key_ref[:, part], table], axis=0), NT) * SCALE
        relative = [content[:, at : at + width] for at in (width, 2 * width)]
        for step in range(STEPS):
            moved = lanes(relative[1], place[step])
            if step == 0:
                score_out[:, part] = jnp.where(seen, content[:, :width] + moved, -jnp.inf)
            else:
                moved = jnp.where(upper[step], moved, lanes(relative[0], place[step]))
                moved_out[step - 1, :, part] = moved + biases[step]


def prob_kernel(block_ref, query_ref, near_ref, far_ref, score_ref, moved_ref, prob_out):
    width, span = query_ref.shape
    parts = head_parts(span)
    group = 3 if len(parts) % 3 == 0 else 1
    other = 1 - lax.rem(block_ref[0], 2)
    for start in range(0, len(parts), group):
        mine = parts[start : start + group]

        def heads(load):
            return jnp.concatenate([load(part) for part in mine], axis=0)

        content = heads(
            lambda part: dot(
                query_ref[:, part],
                jnp.concatenate([near_ref[other, :, part], far_ref[:, part]], axis=0),
                NT,
            )
        ) * SCALE
        scores = [heads(lambda part: score_ref[:, part])]
        for step in range(1, STEPS):
            at = slice((step - 1) * width, step * width)
            scores.append(content[:, at] + heads(lambda part: moved_ref[step - 1, :, part]))
        top = jnp.maximum(jnp.maximum(scores[0], scores[1]), scores[2])
        top = jnp.max(top, axis=1, keepdims=True)
        exps = [jnp.exp(score - top) for score in scores]
        total = jnp.sum(exps[0] + exps[1] + exps[2], axis=1, keepdims=True)
        inverse = 1.0 / total
        for step in range(STEPS):
            prob = exps[step] * inverse
            for at, part in enumerate(mine):
                prob_out[step, :, part] = prob[at * width : (at + 1) * width]


def grads_kernel(
    block_ref, facts_ref, query_ref, grad_ref, key_ref, near_key_ref, near_value_ref, far_key_ref,
    far_value_ref, prob_ref, dprob_ref, turned_ref, table_ref,
    table_out, near_out, far_out, query_out, own_out
):
    width, span = query_ref.shape
    rows = table_out.shape[0]
    table = table_ref[...]
    parts = head_parts(span)
    group = 3 if len(parts) % 3 == 0 else 1
    other = 1 - lax.rem(block_ref[0], 2)
    row, col = iotas(width)
    bases = [facts_ref[step : step + 1, :] for step in range(STEPS)]
    place = [col - row + (rows - 1) - base for base in bases]
    clamps = [place[0] > rows - 1, place[1] > rows - 1, place[2] < 0]
    source = [col + row - (rows - 1) + base for base in bases]
    in_low = [(item >= 0) & (item < width) for item in source]
    in_high = [(item >= -width) & (item < 0) for item in source]
    source = [item & (width - 1) for item in source]
    item_row = lax.broadcasted_iota(jnp.int32, (STEPS * width, rows), 0)
    item_col = lax.broadcasted_iota(jnp.int32, (STEPS * width, rows), 1)
    ends = item_col == jnp.where(item_row < 2 * width, rows - 1, 0)
    ends = jnp.where(ends, 1.0, 0.0).astype(jnp.bfloat16)
    table_sum = jnp.zeros((HEAD_DIM, rows), jnp.float32)

    def many(item):
        return jnp.concatenate([item] * group, axis=0)

    done = []
    for start in range(0, len(parts), group):
        mine = parts[start : start + group]

        def heads(load):
            return jnp.concatenate([load(part) for part in mine], axis=0)

        def products(left_ref, near_ref, far_ref):
            return heads(
                lambda part: dot(
                    left_ref[:, part],
                    jnp.concatenate([near_ref[other, :, part], far_ref[:, part]], axis=0),
                    NT,
                )
            ) * SCALE

        dprob = products(grad_ref, near_value_ref, far_value_ref)
        done.append((start, mine, dprob))
    for start, mine, dprob in done:

        def heads(load):
            return jnp.concatenate([load(part) for part in mine], axis=0)

        probs = [heads(lambda part: prob_ref[step, :, part]) for step in range(STEPS)]
        dprobs = [heads(lambda part: dprob_ref[:, part])]
        for step in range(1, STEPS):
            dprobs.append(dprob[:, (step - 1) * width : step * width])
        mixed = probs[0] * dprobs[0] + probs[1] * dprobs[1] + probs[2] * dprobs[2]
        delta = jnp.sum(mixed, axis=1, keepdims=True)
        dscores = [p * (d - delta) for p, d in zip(probs, dprobs)]
        rounded = [item.astype(jnp.bfloat16) for item in dscores]
        moved = [lanes(item, many(at)) for item, at in zip(dscores, source)]
        below = jnp.where(many(in_low[1]), moved[1], 0.0) + jnp.where(many(in_low[2]), moved[2], 0.0)
        above = jnp.where(many(in_high[0]), moved[0], 0.0) + jnp.where(many(in_high[1]), moved[1], 0.0)
        above = above + jnp.where(many(in_high[2]), moved[2], 0.0)
        clamped = [
            jnp.where(many(mask), item, 0.0).astype(jnp.bfloat16)
            for mask, item in zip(clamps, dscores)
        ]
        clamped = dot(jnp.concatenate(clamped, axis=1), ends)
        relative = (jnp.concatenate([below, above], axis=1) + clamped).astype(jnp.bfloat16)
        for at, part in enumerate(mine):
            here = slice(at * width, (at + 1) * width)
            table_sum = table_sum + dot(turned_ref[part, :], relative[here])
        for at, part in enumerate(mine):
            here = slice(at * width, (at + 1) * width)
            terms = jnp.concatenate([item[here] for item in rounded] + [relative[here]], axis=1)
            weight = jnp.concatenate([item[here].astype(jnp.bfloat16) for item in probs], axis=1)
            keys = [key_ref[:, part], near_key_ref[other, :, part], far_key_ref[:, part], table]
            query_out[:, part] = dot(terms, jnp.concatenate(keys, axis=0)).astype(query_out.dtype)
            by_key = dot(terms[:, : STEPS * width], query_ref[:, part], TN)
            by_value = dot(weight, grad_ref[:, part], TN)
            for slot, item in enumerate((by_key, by_value)):
                own_out[slot, :, part] = item[:width]
                near_out[slot, :, part] = item[width : 2 * width].astype(jnp.bfloat16)
                far_out[slot, :, part] = item[2 * width :].astype(jnp.bfloat16)
    table_out[...] = table_sum.T


def spread_kernel(flipped, pieces_ref, copies_out):
    total = pieces_ref[0]
    for index in range(1, pieces_ref.shape[0]):
        total = total + pieces_ref[index]
    if flipped:
        small = total.shape[0]
        total = jnp.concatenate([total[at : at + 1] for at in reversed(range(small))], axis=0)
    for index in range(copies_out.shape[0]):
        copies_out[index] = total


def final_kernel(own_ref, near_ref, far_ref, table_ref, key_out, value_out, table_out):
    for slot, out in enumerate((key_out, value_out)):
        total = own_ref[slot] + near_ref[slot].astype(jnp.float32) + far_ref[slot].astype(jnp.float32)
        out[...] = total.astype(out.dtype)
    table_out[...] = table_ref[...]


def rings(count, head):
    depth = 16
    columns = count // (2 * depth)
    lead = 9
    planes = []
    for z in range(depth):
        plane = [
            (column * 2 * depth + z * 2 + core) * head + half
            for column in range(columns)
            for core in range(2)
            for half in range(head)
        ]
        far = plane.pop(len(plane) * 9 // 32)
        planes.append(plane + [far])
    lines = [
        [
            (column * 2 * depth + (z + lead) % depth * 2 + core) * head + half
            for z in range(depth)
        ]
        for column in range(columns)
        for core in range(2)
        for half in range(head)
    ]
    return planes, lines


def shards(queries, key_states, value_states, out_grad, rel_table, block_mask, distance_shift):
    count = lax.axis_size("ctx")
    width, span = queries.shape
    rows = rel_table.shape[0]
    heads = span // HEAD_DIM
    block = lax.axis_index("ctx").astype(jnp.int32).reshape(1)
    odd = lax.rem(block[0], 2) == 1
    pairs = [[i, i + 1] for i in range(0, count, 2)]
    ahead = [(i, (i + 2) % count) for i in range(count)]
    one, two, three = (width, span), (2, width, span), (STEPS, width, span)
    bf, f32 = jnp.bfloat16, jnp.float32
    scalar, local = [pltpu.SMEM], [pltpu.VMEM]
    far_value = lax.ppermute(value_states, "ctx", ahead)
    far_key = lax.ppermute(key_states, "ctx", ahead)
    (flip,) = call(flip_kernel, (((rows, rows), bf),), (), [], [], 10, "flip")
    score, moved, dprob, turned, facts, table, key_states, value_states = call(
        own_kernel,
        (
            (one, f32), (two, f32), (one, f32), ((span, width), bf), ((8, width), jnp.int32),
            (rel_table.shape, bf), (one, bf), (one, bf),
        ),
        (
            block, block_mask, distance_shift, queries, out_grad, key_states, value_states,
            rel_table, flip,
        ),
        scalar * 3 + local * 6, [], 3, "own_scores",
    )
    far_key, score = lax.optimization_barrier((far_key, score))
    near_key = lax.all_gather(jnp.where(odd, far_key, key_states), "ctx", axis_index_groups=pairs)
    (prob,) = call(
        prob_kernel,
        ((three, f32),),
        (block, queries, near_key, far_key, score, moved),
        scalar + local * 5, [], 1, "probabilities",
    )
    far_value, prob = lax.optimization_barrier((far_value, prob))
    near_value = lax.all_gather(jnp.where(odd, far_value, value_states), "ctx", axis_index_groups=pairs)
    table_part, near_part, far_part, query_grad, own = call(
        grads_kernel,
        (((rows, HEAD_DIM), f32), (two, bf), (two, bf), (one, bf), (two, f32)),
        (
            block, facts, queries, out_grad, key_states, near_key, near_value, far_key, far_value,
            prob, dprob, turned, table,
        ),
        scalar + local * 12, [], 6, "block_grads",
    )
    planes, lines = rings(count, lax.axis_size("head"))
    small = rows // len(planes[0])
    shape = (len(planes[0]), small, HEAD_DIM)
    table_part, near_part, far_part = lax.optimization_barrier((table_part, near_part, far_part))
    near_part = lax.ppermute(near_part, "ctx", [(i, (i - 1) % count) for i in range(count)])
    pieces = lax.all_to_all(table_part.reshape(shape), AXES, 0, 0, axis_index_groups=planes)
    (copies,) = call(
        functools.partial(spread_kernel, True),
        (((len(lines[0]), small, HEAD_DIM), f32),), (pieces,), local, [], 40, "plane_sum",
    )
    copies, far_part = lax.optimization_barrier((copies, far_part))
    far_part = lax.ppermute(far_part, "ctx", [(i, (i - 2) % count) for i in range(count)])
    pieces = lax.all_to_all(copies, AXES, 0, 0, axis_index_groups=lines)
    (copies,) = call(
        functools.partial(spread_kernel, False), ((shape, f32),), (pieces,), local, [], 4, "line_sum",
    )
    copies = lax.all_to_all(copies, AXES, 0, 0, axis_index_groups=[plane[::-1] for plane in planes])
    key_grad, value_grad, table_grad = call(
        final_kernel,
        ((one, bf), (one, bf), ((rows, HEAD_DIM), f32)),
        (own, near_part, far_part, copies.reshape(rows, HEAD_DIM)),
        local * 4, [], 1, "final_sums",
    )
    return query_grad, key_grad, value_grad, table_grad


def solution(mesh):
    return jax.shard_map(
        shards,
        mesh=mesh,
        in_specs=(
            P("ctx", "head"),
            P("ctx", "head"),
            P("ctx", "head"),
            P("ctx", "head"),
            P(),
            P("ctx", None),
            P("ctx", None),
        ),
        out_specs=(P("ctx", "head"), P("ctx", "head"), P("ctx", "head"), P()),
        check_vma=False,
    )
```

```python
import functools

import jax
import jax.numpy as jnp
from jax import lax
from jax.experimental import pallas as pl
from jax.experimental.pallas import tpu as pltpu
from jax.sharding import PartitionSpec as P

HEAD_DIM = 128
STEPS = 3
AXES = ("ctx", "head")
NN = (((1,), (0,)), ((), ()))
NT = (((1,), (1,)), ((), ()))
TN = (((0,), (0,)), ((), ()))
SCALE = HEAD_DIM ** (-0.5)


def dot(a, b, dims=NN):
    return lax.dot_general(a, b, dims, preferred_element_type=jnp.float32)


def lanes(values, index):
    return jnp.take_along_axis(values, index, axis=1, mode="promise_in_bounds")


def head_parts(span):
    return [slice(at, at + HEAD_DIM) for at in range(0, span, HEAD_DIM)]


def iotas(width):
    row = lax.broadcasted_iota(jnp.int32, (width, width), 0)
    col = lax.broadcasted_iota(jnp.int32, (width, width), 1)
    return row, col


def call(kernel, outs, ins, spaces, scratch, micros, name):
    return pl.pallas_call(
        kernel,
        out_shape=tuple(jax.ShapeDtypeStruct(shape, kind) for shape, kind in outs),
        in_specs=[pl.BlockSpec(memory_space=space) for space in spaces],
        out_specs=(pl.BlockSpec(memory_space=pltpu.VMEM),) * len(outs),
        scratch_shapes=scratch,
        compiler_params=pltpu.CompilerParams(vmem_limit_bytes=32 * 1024 * 1024),
        cost_estimate=pl.CostEstimate(
            flops=micros * 1_000_000_000, bytes_accessed=0, transcendentals=0
        ),
        name=name,
    )(*ins)


def flip_kernel(flip_out):
    row, col = iotas(flip_out.shape[0])
    last = flip_out.shape[0] - 1
    flip_out[...] = jnp.where(row + col == last, 1.0, 0.0).astype(flip_out.dtype)


def own_kernel(
    block_ref, mask_ref, shift_ref, query_ref, grad_ref, key_ref, value_ref, table_ref, flip_ref,
    score_out, moved_out, dprob_out, turned_out, facts_out, table_out, key_out, value_out
):
    width, span = query_ref.shape
    rows = table_ref.shape[0]
    row, col = iotas(width)
    seen = col <= row
    bases = [step * width - shift_ref[0, step] for step in range(STEPS)]
    biases = [
        jnp.where((mask_ref[0, step] == 1) & (block_ref[0] >= step), 0.0, -jnp.inf)
        for step in range(STEPS)
    ]
    line = lax.broadcasted_iota(jnp.int32, facts_out.shape, 0)
    facts = jnp.zeros(facts_out.shape, jnp.int32)
    for step in range(STEPS):
        facts = jnp.where(line == step, bases[step], facts)
    facts_out[...] = facts
    place = [jnp.clip(col - row + (rows - 1) - base, 0, rows - 1) for base in bases]
    upper = [item >= width for item in place]
    place = [item & (width - 1) for item in place]
    table = dot(flip_ref[...], table_ref[...]).astype(jnp.bfloat16)
    table_out[...] = table
    key_out[...] = key_ref[...]
    value_out[...] = value_ref[...]
    for part in head_parts(span):
        query = query_ref[:, part]
        turned_out[part, :] = query.T
        dprob_out[:, part] = dot(grad_ref[:, part], value_ref[:, part], NT) * SCALE
        content = dot(query, jnp.concatenate([key_ref[:, part], table], axis=0), NT) * SCALE
        relative = [content[:, at : at + width] for at in (width, 2 * width)]
        for step in range(STEPS):
            moved = lanes(relative[1], place[step])
            if step == 0:
                score_out[:, part] = jnp.where(seen, content[:, :width] + moved, -jnp.inf)
            else:
                moved = jnp.where(upper[step], moved, lanes(relative[0], place[step]))
                moved_out[step - 1, :, part] = moved + biases[step]


def prob_kernel(block_ref, query_ref, near_ref, far_ref, score_ref, moved_ref, prob_out):
    width, span = query_ref.shape
    parts = head_parts(span)
    group = 3 if len(parts) % 3 == 0 else 1
    other = 1 - lax.rem(block_ref[0], 2)
    for start in range(0, len(parts), group):
        mine = parts[start : start + group]

        def heads(load):
            return jnp.concatenate([load(part) for part in mine], axis=0)

        content = heads(
            lambda part: dot(
                query_ref[:, part],
                jnp.concatenate([near_ref[other, :, part], far_ref[:, part]], axis=0),
                NT,
            )
        ) * SCALE
        scores = [heads(lambda part: score_ref[:, part])]
        for step in range(1, STEPS):
            at = slice((step - 1) * width, step * width)
            scores.append(content[:, at] + heads(lambda part: moved_ref[step - 1, :, part]))
        top = jnp.maximum(jnp.maximum(scores[0], scores[1]), scores[2])
        top = jnp.max(top, axis=1, keepdims=True)
        exps = [jnp.exp(score - top) for score in scores]
        total = jnp.sum(exps[0] + exps[1] + exps[2], axis=1, keepdims=True)
        inverse = 1.0 / total
        for step in range(STEPS):
            prob = exps[step] * inverse
            for at, part in enumerate(mine):
                prob_out[step, :, part] = prob[at * width : (at + 1) * width]


def grads_kernel(
    block_ref, facts_ref, query_ref, grad_ref, key_ref, near_key_ref, near_value_ref, far_key_ref,
    far_value_ref, prob_ref, dprob_ref, turned_ref, table_ref,
    table_out, near_out, far_out, query_out, own_out
):
    width, span = query_ref.shape
    rows = table_out.shape[0]
    table = table_ref[...]
    parts = head_parts(span)
    group = 3 if len(parts) % 3 == 0 else 1
    other = 1 - lax.rem(block_ref[0], 2)
    row, col = iotas(width)
    bases = [facts_ref[step : step + 1, :] for step in range(STEPS)]
    place = [col - row + (rows - 1) - base for base in bases]
    clamps = [place[0] > rows - 1, place[1] > rows - 1, place[2] < 0]
    source = [col + row - (rows - 1) + base for base in bases]
    in_low = [(item >= 0) & (item < width) for item in source]
    in_high = [(item >= -width) & (item < 0) for item in source]
    source = [item & (width - 1) for item in source]
    item_row = lax.broadcasted_iota(jnp.int32, (STEPS * width, rows), 0)
    item_col = lax.broadcasted_iota(jnp.int32, (STEPS * width, rows), 1)
    ends = item_col == jnp.where(item_row < 2 * width, rows - 1, 0)
    ends = jnp.where(ends, 1.0, 0.0).astype(jnp.bfloat16)
    table_sum = jnp.zeros((HEAD_DIM, rows), jnp.float32)

    def many(item):
        return jnp.concatenate([item] * group, axis=0)

    done = []
    for start in range(0, len(parts), group):
        mine = parts[start : start + group]

        def heads(load):
            return jnp.concatenate([load(part) for part in mine], axis=0)

        def products(left_ref, near_ref, far_ref):
            return heads(
                lambda part: dot(
                    left_ref[:, part],
                    jnp.concatenate([near_ref[other, :, part], far_ref[:, part]], axis=0),
                    NT,
                )
            ) * SCALE

        dprob = products(grad_ref, near_value_ref, far_value_ref)
        done.append((start, mine, dprob))
    for start, mine, dprob in done:

        def heads(load):
            return jnp.concatenate([load(part) for part in mine], axis=0)

        probs = [heads(lambda part: prob_ref[step, :, part]) for step in range(STEPS)]
        dprobs = [heads(lambda part: dprob_ref[:, part])]
        for step in range(1, STEPS):
            dprobs.append(dprob[:, (step - 1) * width : step * width])
        mixed = probs[0] * dprobs[0] + probs[1] * dprobs[1] + probs[2] * dprobs[2]
        delta = jnp.sum(mixed, axis=1, keepdims=True)
        dscores = [p * (d - delta) for p, d in zip(probs, dprobs)]
        rounded = [item.astype(jnp.bfloat16) for item in dscores]
        moved = [lanes(item, many(at)) for item, at in zip(dscores, source)]
        below = jnp.where(many(in_low[1]), moved[1], 0.0) + jnp.where(many(in_low[2]), moved[2], 0.0)
        above = jnp.where(many(in_high[0]), moved[0], 0.0) + jnp.where(many(in_high[1]), moved[1], 0.0)
        above = above + jnp.where(many(in_high[2]), moved[2], 0.0)
        clamped = [
            jnp.where(many(mask), item, 0.0).astype(jnp.bfloat16)
            for mask, item in zip(clamps, dscores)
        ]
        clamped = dot(jnp.concatenate(clamped, axis=1), ends)
        relative = (jnp.concatenate([below, above], axis=1) + clamped).astype(jnp.bfloat16)
        for at, part in enumerate(mine):
            here = slice(at * width, (at + 1) * width)
            table_sum = table_sum + dot(turned_ref[part, :], relative[here])
        for at, part in enumerate(mine):
            here = slice(at * width, (at + 1) * width)
            terms = jnp.concatenate([item[here] for item in rounded] + [relative[here]], axis=1)
            weight = jnp.concatenate([item[here].astype(jnp.bfloat16) for item in probs], axis=1)
            keys = [key_ref[:, part], near_key_ref[other, :, part], far_key_ref[:, part], table]
            query_out[:, part] = dot(terms, jnp.concatenate(keys, axis=0)).astype(query_out.dtype)
            by_key = dot(terms[:, : STEPS * width], query_ref[:, part], TN)
            by_value = dot(weight, grad_ref[:, part], TN)
            for slot, item in enumerate((by_key, by_value)):
                own_out[slot, :, part] = item[:width]
                near_out[slot, :, part] = item[width : 2 * width].astype(jnp.bfloat16)
                far_out[slot, :, part] = item[2 * width :].astype(jnp.bfloat16)
    table_out[...] = table_sum.T


def spread_kernel(flipped, pieces_ref, copies_out):
    total = pieces_ref[0]
    for index in range(1, pieces_ref.shape[0]):
        total = total + pieces_ref[index]
    if flipped:
        small = total.shape[0]
        total = jnp.concatenate([total[at : at + 1] for at in reversed(range(small))], axis=0)
    for index in range(copies_out.shape[0]):
        copies_out[index] = total


def final_kernel(own_ref, near_ref, far_ref, table_ref, key_out, value_out, table_out):
    for slot, out in enumerate((key_out, value_out)):
        total = own_ref[slot] + near_ref[slot].astype(jnp.float32) + far_ref[slot].astype(jnp.float32)
        out[...] = total.astype(out.dtype)
    table_out[...] = table_ref[...]


def rings(count, head):
    depth = 16
    columns = count // (2 * depth)
    lead = 11
    planes = []
    for z in range(depth):
        plane = [
            (column * 2 * depth + z * 2 + core) * head + half
            for column in range(columns)
            for core in range(2)
            for half in range(head)
        ]
        far = plane.pop(len(plane) * 9 // 32)
        planes.append(plane + [far])
    lines = [
        [
            (column * 2 * depth + (z + lead) % depth * 2 + core) * head + half
            for z in range(depth)
        ]
        for column in range(columns)
        for core in range(2)
        for half in range(head)
    ]
    return planes, lines


def shards(queries, key_states, value_states, out_grad, rel_table, block_mask, distance_shift):
    count = lax.axis_size("ctx")
    width, span = queries.shape
    rows = rel_table.shape[0]
    heads = span // HEAD_DIM
    block = lax.axis_index("ctx").astype(jnp.int32).reshape(1)
    odd = lax.rem(block[0], 2) == 1
    pairs = [[i, i + 1] for i in range(0, count, 2)]
    ahead = [(i, (i + 2) % count) for i in range(count)]
    one, two, three = (width, span), (2, width, span), (STEPS, width, span)
    bf, f32 = jnp.bfloat16, jnp.float32
    scalar, local = [pltpu.SMEM], [pltpu.VMEM]
    far_value = lax.ppermute(value_states, "ctx", ahead)
    far_key = lax.ppermute(key_states, "ctx", ahead)
    (flip,) = call(flip_kernel, (((rows, rows), bf),), (), [], [], 10, "flip")
    score, moved, dprob, turned, facts, table, key_states, value_states = call(
        own_kernel,
        (
            (one, f32), (two, f32), (one, f32), ((span, width), bf), ((8, width), jnp.int32),
            (rel_table.shape, bf), (one, bf), (one, bf),
        ),
        (
            block, block_mask, distance_shift, queries, out_grad, key_states, value_states,
            rel_table, flip,
        ),
        scalar * 3 + local * 6, [], 3, "own_scores",
    )
    far_key, score = lax.optimization_barrier((far_key, score))
    near_key = lax.all_gather(jnp.where(odd, far_key, key_states), "ctx", axis_index_groups=pairs)
    (prob,) = call(
        prob_kernel,
        ((three, f32),),
        (block, queries, near_key, far_key, score, moved),
        scalar + local * 5, [], 1, "probabilities",
    )
    far_value, prob = lax.optimization_barrier((far_value, prob))
    near_value = lax.all_gather(jnp.where(odd, far_value, value_states), "ctx", axis_index_groups=pairs)
    table_part, near_part, far_part, query_grad, own = call(
        grads_kernel,
        (((rows, HEAD_DIM), f32), (two, bf), (two, bf), (one, bf), (two, f32)),
        (
            block, facts, queries, out_grad, key_states, near_key, near_value, far_key, far_value,
            prob, dprob, turned, table,
        ),
        scalar + local * 12, [], 6, "block_grads",
    )
    planes, lines = rings(count, lax.axis_size("head"))
    small = rows // len(planes[0])
    shape = (len(planes[0]), small, HEAD_DIM)
    table_part, near_part, far_part = lax.optimization_barrier((table_part, near_part, far_part))
    near_part = lax.ppermute(near_part, "ctx", [(i, (i - 1) % count) for i in range(count)])
    pieces = lax.all_to_all(table_part.reshape(shape), AXES, 0, 0, axis_index_groups=planes)
    (copies,) = call(
        functools.partial(spread_kernel, True),
        (((len(lines[0]), small, HEAD_DIM), f32),), (pieces,), local, [], 40, "plane_sum",
    )
    copies, far_part = lax.optimization_barrier((copies, far_part))
    far_part = lax.ppermute(far_part, "ctx", [(i, (i - 2) % count) for i in range(count)])
    pieces = lax.all_to_all(copies, AXES, 0, 0, axis_index_groups=lines)
    (copies,) = call(
        functools.partial(spread_kernel, False), ((shape, f32),), (pieces,), local, [], 4, "line_sum",
    )
    copies = lax.all_to_all(copies, AXES, 0, 0, axis_index_groups=[plane[::-1] for plane in planes])
    key_grad, value_grad, table_grad = call(
        final_kernel,
        ((one, bf), (one, bf), ((rows, HEAD_DIM), f32)),
        (own, near_part, far_part, copies.reshape(rows, HEAD_DIM)),
        local * 4, [], 1, "final_sums",
    )
    return query_grad, key_grad, value_grad, table_grad


def solution(mesh):
    return jax.shard_map(
        shards,
        mesh=mesh,
        in_specs=(
            P("ctx", "head"),
            P("ctx", "head"),
            P("ctx", "head"),
            P("ctx", "head"),
            P(),
            P("ctx", None),
            P("ctx", None),
        ),
        out_specs=(P("ctx", "head"), P("ctx", "head"), P("ctx", "head"), P()),
        check_vma=False,
    )
```

```python
import functools

import jax
import jax.numpy as jnp
from jax import lax
from jax.experimental import pallas as pl
from jax.experimental.pallas import tpu as pltpu
from jax.sharding import PartitionSpec as P

HEAD_DIM = 128
STEPS = 3
AXES = ("ctx", "head")
NN = (((1,), (0,)), ((), ()))
NT = (((1,), (1,)), ((), ()))
TN = (((0,), (0,)), ((), ()))
SCALE = HEAD_DIM ** (-0.5)


def dot(a, b, dims=NN):
    return lax.dot_general(a, b, dims, preferred_element_type=jnp.float32)


def lanes(values, index):
    return jnp.take_along_axis(values, index, axis=1, mode="promise_in_bounds")


def head_parts(span):
    return [slice(at, at + HEAD_DIM) for at in range(0, span, HEAD_DIM)]


def iotas(width):
    row = lax.broadcasted_iota(jnp.int32, (width, width), 0)
    col = lax.broadcasted_iota(jnp.int32, (width, width), 1)
    return row, col


def call(kernel, outs, ins, spaces, scratch, micros, name):
    return pl.pallas_call(
        kernel,
        out_shape=tuple(jax.ShapeDtypeStruct(shape, kind) for shape, kind in outs),
        in_specs=[pl.BlockSpec(memory_space=space) for space in spaces],
        out_specs=(pl.BlockSpec(memory_space=pltpu.VMEM),) * len(outs),
        scratch_shapes=scratch,
        compiler_params=pltpu.CompilerParams(vmem_limit_bytes=32 * 1024 * 1024),
        cost_estimate=pl.CostEstimate(
            flops=micros * 1_000_000_000, bytes_accessed=0, transcendentals=0
        ),
        name=name,
    )(*ins)


def flip_kernel(flip_out):
    row, col = iotas(flip_out.shape[0])
    last = flip_out.shape[0] - 1
    flip_out[...] = jnp.where(row + col == last, 1.0, 0.0).astype(flip_out.dtype)


def own_kernel(
    block_ref, mask_ref, shift_ref, query_ref, grad_ref, key_ref, value_ref, table_ref, flip_ref,
    score_out, moved_out, dprob_out, turned_out, facts_out, table_out, key_out, value_out
):
    width, span = query_ref.shape
    rows = table_ref.shape[0]
    row, col = iotas(width)
    seen = col <= row
    bases = [step * width - shift_ref[0, step] for step in range(STEPS)]
    biases = [
        jnp.where((mask_ref[0, step] == 1) & (block_ref[0] >= step), 0.0, -jnp.inf)
        for step in range(STEPS)
    ]
    line = lax.broadcasted_iota(jnp.int32, facts_out.shape, 0)
    facts = jnp.zeros(facts_out.shape, jnp.int32)
    for step in range(STEPS):
        facts = jnp.where(line == step, bases[step], facts)
    facts_out[...] = facts
    place = [jnp.clip(col - row + (rows - 1) - base, 0, rows - 1) for base in bases]
    upper = [item >= width for item in place]
    place = [item & (width - 1) for item in place]
    table = dot(flip_ref[...], table_ref[...]).astype(jnp.bfloat16)
    table_out[...] = table
    key_out[...] = key_ref[...]
    value_out[...] = value_ref[...]
    for part in head_parts(span):
        query = query_ref[:, part]
        turned_out[part, :] = query.T
        dprob_out[:, part] = dot(grad_ref[:, part], value_ref[:, part], NT) * SCALE
        content = dot(query, jnp.concatenate([key_ref[:, part], table], axis=0), NT) * SCALE
        relative = [content[:, at : at + width] for at in (width, 2 * width)]
        for step in range(STEPS):
            moved = lanes(relative[1], place[step])
            if step == 0:
                score_out[:, part] = jnp.where(seen, content[:, :width] + moved, -jnp.inf)
            else:
                moved = jnp.where(upper[step], moved, lanes(relative[0], place[step]))
                moved_out[step - 1, :, part] = moved + biases[step]


def prob_kernel(block_ref, query_ref, near_ref, far_ref, score_ref, moved_ref, prob_out):
    width, span = query_ref.shape
    parts = head_parts(span)
    group = 3 if len(parts) % 3 == 0 else 1
    other = 1 - lax.rem(block_ref[0], 2)
    for start in range(0, len(parts), group):
        mine = parts[start : start + group]

        def heads(load):
            return jnp.concatenate([load(part) for part in mine], axis=0)

        content = heads(
            lambda part: dot(
                query_ref[:, part],
                jnp.concatenate([near_ref[other, :, part], far_ref[:, part]], axis=0),
                NT,
            )
        ) * SCALE
        scores = [heads(lambda part: score_ref[:, part])]
        for step in range(1, STEPS):
            at = slice((step - 1) * width, step * width)
            scores.append(content[:, at] + heads(lambda part: moved_ref[step - 1, :, part]))
        top = jnp.maximum(jnp.maximum(scores[0], scores[1]), scores[2])
        top = jnp.max(top, axis=1, keepdims=True)
        exps = [jnp.exp(score - top) for score in scores]
        total = jnp.sum(exps[0] + exps[1] + exps[2], axis=1, keepdims=True)
        inverse = 1.0 / total
        for step in range(STEPS):
            prob = exps[step] * inverse
            for at, part in enumerate(mine):
                prob_out[step, :, part] = prob[at * width : (at + 1) * width]


def grads_kernel(
    block_ref, facts_ref, query_ref, grad_ref, key_ref, near_key_ref, near_value_ref, far_key_ref,
    far_value_ref, prob_ref, dprob_ref, turned_ref, table_ref,
    table_out, near_out, far_out, query_out, own_out
):
    width, span = query_ref.shape
    rows = table_out.shape[0]
    table = table_ref[...]
    parts = head_parts(span)
    group = 3 if len(parts) % 3 == 0 else 1
    other = 1 - lax.rem(block_ref[0], 2)
    row, col = iotas(width)
    bases = [facts_ref[step : step + 1, :] for step in range(STEPS)]
    place = [col - row + (rows - 1) - base for base in bases]
    clamps = [place[0] > rows - 1, place[1] > rows - 1, place[2] < 0]
    source = [col + row - (rows - 1) + base for base in bases]
    in_low = [(item >= 0) & (item < width) for item in source]
    in_high = [(item >= -width) & (item < 0) for item in source]
    source = [item & (width - 1) for item in source]
    item_row = lax.broadcasted_iota(jnp.int32, (STEPS * width, rows), 0)
    item_col = lax.broadcasted_iota(jnp.int32, (STEPS * width, rows), 1)
    ends = item_col == jnp.where(item_row < 2 * width, rows - 1, 0)
    ends = jnp.where(ends, 1.0, 0.0).astype(jnp.bfloat16)
    table_sum = jnp.zeros((HEAD_DIM, rows), jnp.float32)

    def many(item):
        return jnp.concatenate([item] * group, axis=0)

    done = []
    for start in range(0, len(parts), group):
        mine = parts[start : start + group]

        def heads(load):
            return jnp.concatenate([load(part) for part in mine], axis=0)

        def products(left_ref, near_ref, far_ref):
            return heads(
                lambda part: dot(
                    left_ref[:, part],
                    jnp.concatenate([near_ref[other, :, part], far_ref[:, part]], axis=0),
                    NT,
                )
            ) * SCALE

        dprob = products(grad_ref, near_value_ref, far_value_ref)
        done.append((start, mine, dprob))
    for start, mine, dprob in done:

        def heads(load):
            return jnp.concatenate([load(part) for part in mine], axis=0)

        probs = [heads(lambda part: prob_ref[step, :, part]) for step in range(STEPS)]
        dprobs = [heads(lambda part: dprob_ref[:, part])]
        for step in range(1, STEPS):
            dprobs.append(dprob[:, (step - 1) * width : step * width])
        mixed = probs[0] * dprobs[0] + probs[1] * dprobs[1] + probs[2] * dprobs[2]
        delta = jnp.sum(mixed, axis=1, keepdims=True)
        dscores = [p * (d - delta) for p, d in zip(probs, dprobs)]
        rounded = [item.astype(jnp.bfloat16) for item in dscores]
        moved = [lanes(item, many(at)) for item, at in zip(dscores, source)]
        below = jnp.where(many(in_low[1]), moved[1], 0.0) + jnp.where(many(in_low[2]), moved[2], 0.0)
        above = jnp.where(many(in_high[0]), moved[0], 0.0) + jnp.where(many(in_high[1]), moved[1], 0.0)
        above = above + jnp.where(many(in_high[2]), moved[2], 0.0)
        clamped = [
            jnp.where(many(mask), item, 0.0).astype(jnp.bfloat16)
            for mask, item in zip(clamps, dscores)
        ]
        clamped = dot(jnp.concatenate(clamped, axis=1), ends)
        relative = (jnp.concatenate([below, above], axis=1) + clamped).astype(jnp.bfloat16)
        for at, part in enumerate(mine):
            here = slice(at * width, (at + 1) * width)
            table_sum = table_sum + dot(turned_ref[part, :], relative[here])
        for at, part in enumerate(mine):
            here = slice(at * width, (at + 1) * width)
            terms = jnp.concatenate([item[here] for item in rounded] + [relative[here]], axis=1)
            weight = jnp.concatenate([item[here].astype(jnp.bfloat16) for item in probs], axis=1)
            keys = [key_ref[:, part], near_key_ref[other, :, part], far_key_ref[:, part], table]
            query_out[:, part] = dot(terms, jnp.concatenate(keys, axis=0)).astype(query_out.dtype)
            by_key = dot(terms[:, : STEPS * width], query_ref[:, part], TN)
            by_value = dot(weight, grad_ref[:, part], TN)
            for slot, item in enumerate((by_key, by_value)):
                own_out[slot, :, part] = item[:width]
                near_out[slot, :, part] = item[width : 2 * width].astype(jnp.bfloat16)
                far_out[slot, :, part] = item[2 * width :].astype(jnp.bfloat16)
    table_out[...] = table_sum.T


def spread_kernel(flipped, pieces_ref, copies_out):
    total = pieces_ref[0]
    for index in range(1, pieces_ref.shape[0]):
        total = total + pieces_ref[index]
    if flipped:
        small = total.shape[0]
        total = jnp.concatenate([total[at : at + 1] for at in reversed(range(small))], axis=0)
    for index in range(copies_out.shape[0]):
        copies_out[index] = total


def final_kernel(own_ref, near_ref, far_ref, table_ref, key_out, value_out, table_out):
    for slot, out in enumerate((key_out, value_out)):
        total = own_ref[slot] + near_ref[slot].astype(jnp.float32) + far_ref[slot].astype(jnp.float32)
        out[...] = total.astype(out.dtype)
    table_out[...] = table_ref[...]


def rings(count, head):
    depth = 16
    columns = count // (2 * depth)
    lead = 11
    planes = []
    for z in range(depth):
        plane = [
            (column * 2 * depth + z * 2 + core) * head + half
            for column in range(columns)
            for core in range(2)
            for half in range(head)
        ]
        far = plane.pop(len(plane) * 9 // 32)
        planes.append(plane + [far])
    lines = [
        [
            (column * 2 * depth + (z + lead) % depth * 2 + core) * head + half
            for z in range(depth)
        ]
        for column in range(columns)
        for core in range(2)
        for half in range(head)
    ]
    return planes, lines


def shards(queries, key_states, value_states, out_grad, rel_table, block_mask, distance_shift):
    count = lax.axis_size("ctx")
    width, span = queries.shape
    rows = rel_table.shape[0]
    heads = span // HEAD_DIM
    block = lax.axis_index("ctx").astype(jnp.int32).reshape(1)
    odd = lax.rem(block[0], 2) == 1
    pairs = [[i, i + 1] for i in range(0, count, 2)]
    ahead = [(i, (i + 2) % count) for i in range(count)]
    one, two, three = (width, span), (2, width, span), (STEPS, width, span)
    bf, f32 = jnp.bfloat16, jnp.float32
    scalar, local = [pltpu.SMEM], [pltpu.VMEM]
    far_value = lax.ppermute(value_states, "ctx", ahead)
    far_key = lax.ppermute(key_states, "ctx", ahead)
    (flip,) = call(flip_kernel, (((rows, rows), bf),), (), [], [], 10, "flip")
    score, moved, dprob, turned, facts, table, key_states, value_states = call(
        own_kernel,
        (
            (one, f32), (two, f32), (one, f32), ((span, width), bf), ((8, width), jnp.int32),
            (rel_table.shape, bf), (one, bf), (one, bf),
        ),
        (
            block, block_mask, distance_shift, queries, out_grad, key_states, value_states,
            rel_table, flip,
        ),
        scalar * 3 + local * 6, [], 3, "own_scores",
    )
    far_key, score = lax.optimization_barrier((far_key, score))
    near_key = lax.all_gather(jnp.where(odd, far_key, key_states), "ctx", axis_index_groups=pairs)
    (prob,) = call(
        prob_kernel,
        ((three, f32),),
        (block, queries, near_key, far_key, score, moved),
        scalar + local * 5, [], 1, "probabilities",
    )
    far_value, prob = lax.optimization_barrier((far_value, prob))
    near_value = lax.all_gather(jnp.where(odd, far_value, value_states), "ctx", axis_index_groups=pairs)
    table_part, near_part, far_part, query_grad, own = call(
        grads_kernel,
        (((rows, HEAD_DIM), f32), (two, bf), (two, bf), (one, bf), (two, f32)),
        (
            block, facts, queries, out_grad, key_states, near_key, near_value, far_key, far_value,
            prob, dprob, turned, table,
        ),
        scalar + local * 12, [], 6, "block_grads",
    )
    planes, lines = rings(count, lax.axis_size("head"))
    small = rows // len(planes[0])
    shape = (len(planes[0]), small, HEAD_DIM)
    table_part, near_part, far_part = lax.optimization_barrier((table_part, near_part, far_part))
    near_part = lax.ppermute(near_part, "ctx", [(i, (i - 1) % count) for i in range(count)])
    pieces = lax.all_to_all(table_part.reshape(shape), AXES, 0, 0, axis_index_groups=planes)
    (copies,) = call(
        functools.partial(spread_kernel, True),
        (((len(lines[0]), small, HEAD_DIM), f32),), (pieces,), local, [], 40, "plane_sum",
    )
    copies, far_part = lax.optimization_barrier((copies, far_part))
    far_part = lax.ppermute(far_part, "ctx", [(i, (i - 2) % count) for i in range(count)])
    pieces = lax.all_to_all(copies, AXES, 0, 0, axis_index_groups=lines)
    (copies,) = call(
        functools.partial(spread_kernel, False), ((shape, f32),), (pieces,), local, [], 12, "line_sum",
    )
    copies = lax.all_to_all(copies, AXES, 0, 0, axis_index_groups=[plane[::-1] for plane in planes])
    key_grad, value_grad, table_grad = call(
        final_kernel,
        ((one, bf), (one, bf), ((rows, HEAD_DIM), f32)),
        (own, near_part, far_part, copies.reshape(rows, HEAD_DIM)),
        local * 4, [], 1, "final_sums",
    )
    return query_grad, key_grad, value_grad, table_grad


def solution(mesh):
    return jax.shard_map(
        shards,
        mesh=mesh,
        in_specs=(
            P("ctx", "head"),
            P("ctx", "head"),
            P("ctx", "head"),
            P("ctx", "head"),
            P(),
            P("ctx", None),
            P("ctx", None),
        ),
        out_specs=(P("ctx", "head"), P("ctx", "head"), P("ctx", "head"), P()),
        check_vma=False,
    )
```

```python
import functools

import jax
import jax.numpy as jnp
from jax import lax
from jax.experimental import pallas as pl
from jax.experimental.pallas import tpu as pltpu
from jax.sharding import PartitionSpec as P

HEAD_DIM = 128
STEPS = 3
AXES = ("ctx", "head")
NN = (((1,), (0,)), ((), ()))
NT = (((1,), (1,)), ((), ()))
TN = (((0,), (0,)), ((), ()))
SCALE = HEAD_DIM ** (-0.5)


def dot(a, b, dims=NN):
    return lax.dot_general(a, b, dims, preferred_element_type=jnp.float32)


def lanes(values, index):
    return jnp.take_along_axis(values, index, axis=1, mode="promise_in_bounds")


def head_parts(span):
    return [slice(at, at + HEAD_DIM) for at in range(0, span, HEAD_DIM)]


def iotas(width):
    row = lax.broadcasted_iota(jnp.int32, (width, width), 0)
    col = lax.broadcasted_iota(jnp.int32, (width, width), 1)
    return row, col


def call(kernel, outs, ins, spaces, scratch, micros, name):
    return pl.pallas_call(
        kernel,
        out_shape=tuple(jax.ShapeDtypeStruct(shape, kind) for shape, kind in outs),
        in_specs=[pl.BlockSpec(memory_space=space) for space in spaces],
        out_specs=(pl.BlockSpec(memory_space=pltpu.VMEM),) * len(outs),
        scratch_shapes=scratch,
        compiler_params=pltpu.CompilerParams(vmem_limit_bytes=32 * 1024 * 1024),
        cost_estimate=pl.CostEstimate(
            flops=micros * 1_000_000_000, bytes_accessed=0, transcendentals=0
        ),
        name=name,
    )(*ins)


def flip_kernel(flip_out):
    row, col = iotas(flip_out.shape[0])
    last = flip_out.shape[0] - 1
    flip_out[...] = jnp.where(row + col == last, 1.0, 0.0).astype(flip_out.dtype)


def own_kernel(
    block_ref, mask_ref, shift_ref, query_ref, grad_ref, key_ref, value_ref, table_ref, flip_ref,
    score_out, moved_out, dprob_out, turned_out, facts_out, table_out, key_out, value_out
):
    width, span = query_ref.shape
    rows = table_ref.shape[0]
    row, col = iotas(width)
    seen = col <= row
    bases = [step * width - shift_ref[0, step] for step in range(STEPS)]
    biases = [
        jnp.where((mask_ref[0, step] == 1) & (block_ref[0] >= step), 0.0, -jnp.inf)
        for step in range(STEPS)
    ]
    line = lax.broadcasted_iota(jnp.int32, facts_out.shape, 0)
    facts = jnp.zeros(facts_out.shape, jnp.int32)
    for step in range(STEPS):
        facts = jnp.where(line == step, bases[step], facts)
    facts_out[...] = facts
    place = [jnp.clip(col - row + (rows - 1) - base, 0, rows - 1) for base in bases]
    upper = [item >= width for item in place]
    place = [item & (width - 1) for item in place]
    table = dot(flip_ref[...], table_ref[...]).astype(jnp.bfloat16)
    table_out[...] = table
    key_out[...] = key_ref[...]
    value_out[...] = value_ref[...]
    for part in head_parts(span):
        query = query_ref[:, part]
        turned_out[part, :] = query.T
        dprob_out[:, part] = dot(grad_ref[:, part], value_ref[:, part], NT) * SCALE
        content = dot(query, jnp.concatenate([key_ref[:, part], table], axis=0), NT) * SCALE
        relative = [content[:, at : at + width] for at in (width, 2 * width)]
        for step in range(STEPS):
            moved = lanes(relative[1], place[step])
            if step == 0:
                score_out[:, part] = jnp.where(seen, content[:, :width] + moved, -jnp.inf)
            else:
                moved = jnp.where(upper[step], moved, lanes(relative[0], place[step]))
                moved_out[step - 1, :, part] = moved + biases[step]


def prob_kernel(block_ref, query_ref, near_ref, far_ref, score_ref, moved_ref, prob_out):
    width, span = query_ref.shape
    parts = head_parts(span)
    group = 3 if len(parts) % 3 == 0 else 1
    other = 1 - lax.rem(block_ref[0], 2)
    for start in range(0, len(parts), group):
        mine = parts[start : start + group]

        def heads(load):
            return jnp.concatenate([load(part) for part in mine], axis=0)

        content = heads(
            lambda part: dot(
                query_ref[:, part],
                jnp.concatenate([near_ref[other, :, part], far_ref[:, part]], axis=0),
                NT,
            )
        ) * SCALE
        scores = [heads(lambda part: score_ref[:, part])]
        for step in range(1, STEPS):
            at = slice((step - 1) * width, step * width)
            scores.append(content[:, at] + heads(lambda part: moved_ref[step - 1, :, part]))
        top = jnp.maximum(jnp.maximum(scores[0], scores[1]), scores[2])
        top = jnp.max(top, axis=1, keepdims=True)
        exps = [jnp.exp(score - top) for score in scores]
        total = jnp.sum(exps[0] + exps[1] + exps[2], axis=1, keepdims=True)
        inverse = 1.0 / total
        for step in range(STEPS):
            prob = exps[step] * inverse
            for at, part in enumerate(mine):
                prob_out[step, :, part] = prob[at * width : (at + 1) * width]


def grads_kernel(
    block_ref, facts_ref, query_ref, grad_ref, key_ref, near_key_ref, near_value_ref, far_key_ref,
    far_value_ref, prob_ref, dprob_ref, turned_ref, table_ref,
    table_out, near_out, far_out, query_out, own_out
):
    width, span = query_ref.shape
    rows = table_out.shape[0]
    table = table_ref[...]
    parts = head_parts(span)
    group = 3 if len(parts) % 3 == 0 else 1
    other = 1 - lax.rem(block_ref[0], 2)
    row, col = iotas(width)
    bases = [facts_ref[step : step + 1, :] for step in range(STEPS)]
    place = [col - row + (rows - 1) - base for base in bases]
    clamps = [place[0] > rows - 1, place[1] > rows - 1, place[2] < 0]
    source = [col + row - (rows - 1) + base for base in bases]
    in_low = [(item >= 0) & (item < width) for item in source]
    in_high = [(item >= -width) & (item < 0) for item in source]
    source = [item & (width - 1) for item in source]
    item_row = lax.broadcasted_iota(jnp.int32, (STEPS * width, rows), 0)
    item_col = lax.broadcasted_iota(jnp.int32, (STEPS * width, rows), 1)
    ends = item_col == jnp.where(item_row < 2 * width, rows - 1, 0)
    ends = jnp.where(ends, 1.0, 0.0).astype(jnp.bfloat16)
    table_sum = jnp.zeros((HEAD_DIM, rows), jnp.float32)

    def many(item):
        return jnp.concatenate([item] * group, axis=0)

    done = []
    for start in range(0, len(parts), group):
        mine = parts[start : start + group]

        def heads(load):
            return jnp.concatenate([load(part) for part in mine], axis=0)

        def products(left_ref, near_ref, far_ref):
            return heads(
                lambda part: dot(
                    left_ref[:, part],
                    jnp.concatenate([near_ref[other, :, part], far_ref[:, part]], axis=0),
                    NT,
                )
            ) * SCALE

        dprob = products(grad_ref, near_value_ref, far_value_ref)
        done.append((start, mine, dprob))
    for start, mine, dprob in done:

        def heads(load):
            return jnp.concatenate([load(part) for part in mine], axis=0)

        probs = [heads(lambda part: prob_ref[step, :, part]) for step in range(STEPS)]
        dprobs = [heads(lambda part: dprob_ref[:, part])]
        for step in range(1, STEPS):
            dprobs.append(dprob[:, (step - 1) * width : step * width])
        mixed = probs[0] * dprobs[0] + probs[1] * dprobs[1] + probs[2] * dprobs[2]
        delta = jnp.sum(mixed, axis=1, keepdims=True)
        dscores = [p * (d - delta) for p, d in zip(probs, dprobs)]
        rounded = [item.astype(jnp.bfloat16) for item in dscores]
        moved = [lanes(item, many(at)) for item, at in zip(dscores, source)]
        below = jnp.where(many(in_low[1]), moved[1], 0.0) + jnp.where(many(in_low[2]), moved[2], 0.0)
        above = jnp.where(many(in_high[0]), moved[0], 0.0) + jnp.where(many(in_high[1]), moved[1], 0.0)
        above = above + jnp.where(many(in_high[2]), moved[2], 0.0)
        clamped = [
            jnp.where(many(mask), item, 0.0).astype(jnp.bfloat16)
            for mask, item in zip(clamps, dscores)
        ]
        clamped = dot(jnp.concatenate(clamped, axis=1), ends)
        relative = (jnp.concatenate([below, above], axis=1) + clamped).astype(jnp.bfloat16)
        for at, part in enumerate(mine):
            here = slice(at * width, (at + 1) * width)
            table_sum = table_sum + dot(turned_ref[part, :], relative[here])
        for at, part in enumerate(mine):
            here = slice(at * width, (at + 1) * width)
            terms = jnp.concatenate([item[here] for item in rounded] + [relative[here]], axis=1)
            weight = jnp.concatenate([item[here].astype(jnp.bfloat16) for item in probs], axis=1)
            keys = [key_ref[:, part], near_key_ref[other, :, part], far_key_ref[:, part], table]
            query_out[:, part] = dot(terms, jnp.concatenate(keys, axis=0)).astype(query_out.dtype)
            by_key = dot(terms[:, : STEPS * width], query_ref[:, part], TN)
            by_value = dot(weight, grad_ref[:, part], TN)
            for slot, item in enumerate((by_key, by_value)):
                own_out[slot, :, part] = item[:width]
                near_out[slot, :, part] = item[width : 2 * width].astype(jnp.bfloat16)
                far_out[slot, :, part] = item[2 * width :].astype(jnp.bfloat16)
    table_out[...] = table_sum.T


def spread_kernel(flipped, pieces_ref, copies_out):
    total = pieces_ref[0]
    for index in range(1, pieces_ref.shape[0]):
        total = total + pieces_ref[index]
    if flipped:
        small = total.shape[0]
        total = jnp.concatenate([total[at : at + 1] for at in reversed(range(small))], axis=0)
    for index in range(copies_out.shape[0]):
        copies_out[index] = total


def final_kernel(own_ref, near_ref, far_ref, table_ref, key_out, value_out, table_out):
    for slot, out in enumerate((key_out, value_out)):
        total = own_ref[slot] + near_ref[slot].astype(jnp.float32) + far_ref[slot].astype(jnp.float32)
        out[...] = total.astype(out.dtype)
    table_out[...] = table_ref[...]


def rings(count, head):
    depth = 16
    columns = count // (2 * depth)
    planes = []
    for z in range(depth):
        plane = [
            (column * 2 * depth + z * 2 + core) * head + half
            for column in range(columns)
            for core in range(2)
            for half in range(head)
        ]
        far = plane.pop(len(plane) * 9 // 32)
        planes.append(plane + [far])
    lines = [
        [
            (column * 2 * depth + z * 2 + core) * head + half
            for z in (11, 0, 15, 1, 14, 2, 13, 3, 12, 4, 5, 10, 6, 9, 7, 8)
        ]
        for column in range(columns)
        for core in range(2)
        for half in range(head)
    ]
    return planes, lines


def shards(queries, key_states, value_states, out_grad, rel_table, block_mask, distance_shift):
    count = lax.axis_size("ctx")
    width, span = queries.shape
    rows = rel_table.shape[0]
    heads = span // HEAD_DIM
    block = lax.axis_index("ctx").astype(jnp.int32).reshape(1)
    odd = lax.rem(block[0], 2) == 1
    pairs = [[i, i + 1] for i in range(0, count, 2)]
    ahead = [(i, (i + 2) % count) for i in range(count)]
    one, two, three = (width, span), (2, width, span), (STEPS, width, span)
    bf, f32 = jnp.bfloat16, jnp.float32
    scalar, local = [pltpu.SMEM], [pltpu.VMEM]
    far_value = lax.ppermute(value_states, "ctx", ahead)
    far_key = lax.ppermute(key_states, "ctx", ahead)
    (flip,) = call(flip_kernel, (((rows, rows), bf),), (), [], [], 10, "flip")
    score, moved, dprob, turned, facts, table, key_states, value_states = call(
        own_kernel,
        (
            (one, f32), (two, f32), (one, f32), ((span, width), bf), ((8, width), jnp.int32),
            (rel_table.shape, bf), (one, bf), (one, bf),
        ),
        (
            block, block_mask, distance_shift, queries, out_grad, key_states, value_states,
            rel_table, flip,
        ),
        scalar * 3 + local * 6, [], 3, "own_scores",
    )
    far_key, score = lax.optimization_barrier((far_key, score))
    near_key = lax.all_gather(jnp.where(odd, far_key, key_states), "ctx", axis_index_groups=pairs)
    (prob,) = call(
        prob_kernel,
        ((three, f32),),
        (block, queries, near_key, far_key, score, moved),
        scalar + local * 5, [], 1, "probabilities",
    )
    far_value, prob = lax.optimization_barrier((far_value, prob))
    near_value = lax.all_gather(jnp.where(odd, far_value, value_states), "ctx", axis_index_groups=pairs)
    table_part, near_part, far_part, query_grad, own = call(
        grads_kernel,
        (((rows, HEAD_DIM), f32), (two, bf), (two, bf), (one, bf), (two, f32)),
        (
            block, facts, queries, out_grad, key_states, near_key, near_value, far_key, far_value,
            prob, dprob, turned, table,
        ),
        scalar + local * 12, [], 6, "block_grads",
    )
    planes, lines = rings(count, lax.axis_size("head"))
    small = rows // len(planes[0])
    shape = (len(planes[0]), small, HEAD_DIM)
    table_part, near_part, far_part = lax.optimization_barrier((table_part, near_part, far_part))
    near_part = lax.ppermute(near_part, "ctx", [(i, (i - 1) % count) for i in range(count)])
    pieces = lax.all_to_all(table_part.reshape(shape), AXES, 0, 0, axis_index_groups=planes)
    (copies,) = call(
        functools.partial(spread_kernel, True),
        (((len(lines[0]), small, HEAD_DIM), f32),), (pieces,), local, [], 40, "plane_sum",
    )
    copies, far_part = lax.optimization_barrier((copies, far_part))
    far_part = lax.ppermute(far_part, "ctx", [(i, (i - 2) % count) for i in range(count)])
    pieces = lax.all_to_all(copies, AXES, 0, 0, axis_index_groups=lines)
    (copies,) = call(
        functools.partial(spread_kernel, False), ((shape, f32),), (pieces,), local, [], 12, "line_sum",
    )
    copies = lax.all_to_all(copies, AXES, 0, 0, axis_index_groups=[plane[::-1] for plane in planes])
    key_grad, value_grad, table_grad = call(
        final_kernel,
        ((one, bf), (one, bf), ((rows, HEAD_DIM), f32)),
        (own, near_part, far_part, copies.reshape(rows, HEAD_DIM)),
        local * 4, [], 1, "final_sums",
    )
    return query_grad, key_grad, value_grad, table_grad


def solution(mesh):
    return jax.shard_map(
        shards,
        mesh=mesh,
        in_specs=(
            P("ctx", "head"),
            P("ctx", "head"),
            P("ctx", "head"),
            P("ctx", "head"),
            P(),
            P("ctx", None),
            P("ctx", None),
        ),
        out_specs=(P("ctx", "head"), P("ctx", "head"), P("ctx", "head"), P()),
        check_vma=False,
    )
```
